32 devices in a mesh: ctx: 4 (over z), tis: 2 (over y), rep: 4 (over x, core).
Axes of the slice: x: 2, y: 2, z: 4, core: 2. Of those that a mesh axis runs over, the one named last changes fastest.
Arguments:
- donor_feat: bfloat16 [4, 64, 256], P('rep', 'ctx'), may hold values from -6 to 6
- acceptor_feat: bfloat16 [4, 64, 256], P('rep', 'ctx'), may hold values from -6 to 6
- donor_pos: int32 [4, 64], P('rep', 'ctx'), may hold values from 0 to 65535
- acceptor_pos: int32 [4, 64], P('rep'), may hold values from 0 to 65535
- pair_mask: int32 [4, 64, 80], P('rep', 'ctx'), may hold values from 0 to 1
- targets: int32 [4, 64, 8], P('rep', 'ctx', 'tis'), may hold values from 0 to 80, as said below
- dist_table: bfloat16 [128, 256], replicated, may hold values from -3 to 3
- hidden_weights: bfloat16 [8, 256, 512], P('tis'), may hold values from -0.375 to 0.375
- output_weights: bfloat16 [8, 512], P('tis')
Outputs:
- donor_loss: float32 [4, 64, 8], P('rep', 'ctx', 'tis')
- grad_hidden: float32 [8, 256, 512], P('tis', ('ctx', 'rep'))
- grad_acceptor: float32 [4, 64, 256], P('rep', 'ctx')
The draws below stay inside these ranges and needn't reach their ends.
Inputs may be any that keep to these rules, and one draw needn't show every extreme that they name: `targets`: each target is a valid slot of its donor, or 80 for no splice.
All inputs are finite; a program needn't handle non-finite values.
Results may differ from the reference program's by a relative error of at most 0.002.
The reference program's roundings to bfloat16 on the way (of `pair`, `act` and `grad_hid`) count: a program that leaves them out, or rounds other values in their place, can miss the bound.
Values may be sent and summed in bfloat16 or wider, within the bound.
No kernel may reach another device: no remote copies, remote signals or barrier semaphores. Data moves between devices by JAX's collectives and lax.ppermute only.
A program may use at most 64 MiB of HBM per device.

```python
import math
import jax
import jax.numpy as jnp
from jax import lax

F = 256
H = 512
DON_BLK = 16
ACC_BLK = 16
BLOCK_BP = 65536
SPAN_BLOCKS = 4
BIN_BP = 2048
BINS = 128
SLOTS = 80
TISSUES = 8
SEQS = 4
DONORS = 64
ACCEPTORS = 64


def layout_draw(key):
    key_don = jax.random.fold_in(key, 11)
    key_acc = jax.random.fold_in(key, 12)
    key_mask = jax.random.fold_in(key, 13)
    key_goal = jax.random.fold_in(key, 14)
    nblocks = DONORS // DON_BLK
    reach = SPAN_BLOCKS + 1
    dpos = jax.random.randint(key_don, (SEQS, DONORS), 0, BLOCK_BP).astype(jnp.int32)
    dpos = dpos.at[0, 0].set(0).at[0, 1].set(BLOCK_BP - 1)
    apos = jax.random.randint(key_acc, (SEQS, ACCEPTORS), 0, BLOCK_BP).astype(jnp.int32)
    apos = apos.at[0, 0].set(0).at[0, 1].set(BLOCK_BP - 1)
    mask = (jax.random.randint(key_mask, (SEQS, DONORS, SLOTS), 0, 5) > 0).astype(jnp.int32)
    blocked = apos.reshape(SEQS, nblocks, ACC_BLK)
    padded = jnp.concatenate([blocked, jnp.zeros((SEQS, SPAN_BLOCKS, ACC_BLK), jnp.int32)], axis=1)
    pos_win = jnp.stack([padded[:, offset:offset + nblocks] for offset in range(reach)], axis=2).reshape(SEQS, nblocks, SLOTS)
    slot_block = jnp.arange(SLOTS, dtype=jnp.int32) // ACC_BLK
    inchain = jnp.arange(nblocks, dtype=jnp.int32)[:, None] + slot_block[None, :] < nblocks
    dist = slot_block * BLOCK_BP + pos_win[:, :, None, :] - dpos.reshape(SEQS, nblocks, DON_BLK)[..., None]
    valid = (mask.reshape(SEQS, nblocks, DON_BLK, SLOTS) > 0) & (dist > 0) & (dist <= SPAN_BLOCKS * BLOCK_BP) & inchain[None, :, None, :]
    valid = valid.reshape(SEQS, DONORS, 1, SLOTS)
    allowed = jnp.concatenate([jnp.broadcast_to(valid, (SEQS, DONORS, TISSUES, SLOTS)), jnp.ones((SEQS, DONORS, TISSUES, 1), bool)], axis=-1)
    scores = jax.random.randint(key_goal, (SEQS, DONORS, TISSUES, SLOTS + 1), 0, 2 ** 20).astype(jnp.int32)
    scores = scores * (SLOTS + 1) + jnp.arange(SLOTS + 1, dtype=jnp.int32)
    scores = jnp.where(allowed, scores, -1)
    goal = lax.top_k(scores, 1)[1][..., 0].astype(jnp.int32)
    return (dpos, apos, mask, goal)


def draw_donor_pos(key, part):
    return layout_draw(key)[0]


def draw_acceptor_pos(key, part):
    return layout_draw(key)[1]


def draw_pair_mask(key, part):
    return layout_draw(key)[2]


def draw_targets(key, part):
    return layout_draw(key)[3]


def draw_output_weights(key, part):
    values = jax.random.normal(jax.random.fold_in(key, 23), (TISSUES, H), jnp.float32)
    return (values * 2.0 / math.sqrt(H)).astype(jnp.bfloat16)


def level_of(key, dims, shards, smallest, high):
    level = 1.0
    for position, parts in shards:
        heights = jax.random.uniform(jax.random.fold_in(jax.random.fold_in(key, 6), position), (parts,), jnp.float32, smallest / len(shards), high / len(shards))
        level = level * jnp.repeat(jnp.exp(heights), dims[position] // parts).reshape((-1,) + (1,) * (len(dims) - 1 - position))
    return level


def noise(key, extent, spread, limit, cuts=(), held_as=jnp.bfloat16):
    result = spread * jax.random.normal(key, extent, jnp.float32)
    if cuts:
        result = result * level_of(key, extent, cuts, -0.22, 0.18)
    return jnp.clip(result, -limit, limit).astype(held_as)


def setup_inputs(seed: int = 0) -> dict:
    key_list = jax.random.split(jax.random.key(seed), 10)
    return {
        "donor_feat": noise(key_list[0], (SEQS, DONORS, F), 1.0, 6.0, ((0, 4), (1, 4))),
        "acceptor_feat": noise(key_list[1], (SEQS, ACCEPTORS, F), 1.0, 6.0, ((0, 4), (1, 4))),
        "donor_pos": draw_donor_pos(jax.random.fold_in(key_list[9], 71), 0),
        "acceptor_pos": draw_acceptor_pos(jax.random.fold_in(key_list[9], 71), 0),
        "pair_mask": draw_pair_mask(jax.random.fold_in(key_list[9], 71), 0),
        "targets": draw_targets(jax.random.fold_in(key_list[9], 71), 0),
        "dist_table": noise(key_list[6], (BINS, F), 0.5, 3.0),
        "hidden_weights": noise(key_list[7], (TISSUES, F, H), F ** -0.5, 0.375, ((0, 2),)),
        "output_weights": draw_output_weights(jax.random.fold_in(key_list[9], 71), 0),
    }


def silu_grad(values):
    sig = jax.nn.sigmoid(values)
    return sig * (1.0 + values * (1.0 - sig))

def reference(donor_feat, acceptor_feat, donor_pos, acceptor_pos, pair_mask, targets, dist_table, hidden_weights, output_weights):
    nblocks = DONORS // DON_BLK
    reach = SPAN_BLOCKS + 1

    def windows(stacked):
        padding = jnp.zeros((stacked.shape[0], SPAN_BLOCKS) + stacked.shape[2:], stacked.dtype)
        padded = jnp.concatenate([stacked, padding], axis=1)
        return jnp.stack([padded[:, offset:offset + nblocks] for offset in range(reach)], axis=2)
    acc_win = windows(acceptor_feat.reshape(SEQS, nblocks, ACC_BLK, F)).reshape(SEQS, nblocks, SLOTS, F)
    pos_win = windows(acceptor_pos.reshape(SEQS, nblocks, ACC_BLK)).reshape(SEQS, nblocks, SLOTS)
    slot_block = jnp.arange(SLOTS, dtype=jnp.int32) // ACC_BLK
    block_ids = jnp.arange(nblocks, dtype=jnp.int32)
    inchain = block_ids[:, None] + slot_block[None, :] < nblocks
    dpos = donor_pos.reshape(SEQS, nblocks, DON_BLK)
    dist = slot_block * BLOCK_BP + pos_win[:, :, None, :] - dpos[..., None]
    valid = (pair_mask.reshape(SEQS, nblocks, DON_BLK, SLOTS) > 0) & (dist > 0) & (dist <= SPAN_BLOCKS * BLOCK_BP) & inchain[None, :, None, :]
    bins = jnp.clip((dist - 1) // BIN_BP, 0, BINS - 1)
    table = dist_table.astype(jnp.float32)[bins]
    pre = donor_feat.astype(jnp.float32).reshape(SEQS, nblocks, DON_BLK, 1, F) + acc_win.astype(jnp.float32)[:, :, None] + table
    pair = jax.nn.silu(pre).astype(jnp.bfloat16)
    flat = pair.reshape(-1, F)
    goals = jnp.moveaxis(targets.reshape(SEQS, nblocks, DON_BLK, TISSUES), -1, 0)

    def tissue_step(grad_pair, inputs):
        w_in, w_out, goal = inputs
        hid = jnp.dot(flat, w_in, preferred_element_type=jnp.float32)
        act = jax.nn.silu(hid).astype(jnp.bfloat16)
        logits = jnp.dot(act, w_out, preferred_element_type=jnp.float32).reshape(SEQS, nblocks, DON_BLK, SLOTS)
        masked = jnp.where(valid, logits, -jnp.inf)
        top = jnp.maximum(lax.optimization_barrier(jnp.max(masked, axis=-1)), 0.0)
        expo = jnp.exp(masked - top[..., None])
        total = lax.optimization_barrier(jnp.sum(expo, axis=-1)) + jnp.exp(-top)
        picked = jnp.take_along_axis(logits, jnp.minimum(goal, SLOTS - 1)[..., None], axis=-1)[..., 0]
        picked = jnp.where(goal == SLOTS, 0.0, picked)
        loss = top + jnp.log(total) - picked
        onehot = (goal[..., None] == jnp.arange(SLOTS, dtype=jnp.int32)).astype(jnp.float32)
        grad_logits = expo / total[..., None] - onehot
        grad_act = grad_logits.reshape(-1)[:, None] * w_out.astype(jnp.float32)[None, :]
        grad_hid = (grad_act * silu_grad(hid)).astype(jnp.bfloat16)
        grad_w = jnp.dot(flat.T, grad_hid, preferred_element_type=jnp.float32)
        grad_pair = grad_pair + jnp.dot(grad_hid, w_in.T, preferred_element_type=jnp.float32)
        return (grad_pair, (loss, grad_w))
    start = jnp.zeros((flat.shape[0], F), jnp.float32)
    grad_pair, (losses, grad_hidden) = lax.scan(tissue_step, start, (hidden_weights, output_weights, goals))
    grad_pre = grad_pair.reshape(SEQS, nblocks, DON_BLK, SLOTS, F) * silu_grad(pre)
    contrib = lax.optimization_barrier(jnp.sum(grad_pre, axis=2)).reshape(SEQS, nblocks, reach, ACC_BLK, F)
    grad_acc = contrib[:, :, 0]
    for offset in range(1, reach):
        moved = jnp.concatenate([jnp.zeros((SEQS, offset, ACC_BLK, F), jnp.float32), contrib[:, :nblocks - offset, offset]], axis=1)
        grad_acc = grad_acc + moved
    donor_loss = jnp.moveaxis(losses, 0, -1).reshape(SEQS, DONORS, TISSUES)
    return (donor_loss, grad_hidden, grad_acc.reshape(SEQS, ACCEPTORS, F))
```

```python
import functools

import jax
import jax.numpy as jnp
from jax import lax
from jax.experimental import pallas as pl
from jax.experimental.pallas import tpu as pltpu
from jax.sharding import PartitionSpec as P

BLOCK_BP = 65536
SPAN_BLOCKS = 4
BIN_BP = 2048
BINS = 128
LANES = 128


def passed_along(value, axis, steps):
    count = lax.axis_size(axis)
    first, last = (max(0, -steps), min(count, count - steps))
    return lax.ppermute(value, axis, [(source, source + steps) for source in range(first, last)])


def swapped(value, axis, bits):
    return lax.ppermute(value, axis, [(i, i ^ bits) for i in range(lax.axis_size(axis))])


def silu_grad(values):
    sig = jax.nn.sigmoid(values)
    return sig * (1.0 + values * (1.0 - sig))


def general(
    donor_feat,
    acceptor_feat,
    donor_pos,
    acceptor_pos,
    pair_mask,
    targets,
    dist_table,
    hidden_weights,
    output_weights,
):
    seq_dev, don_blk, width = donor_feat.shape
    acc_blk = acceptor_feat.shape[1]
    blocks = lax.axis_size("ctx")
    reach = SPAN_BLOCKS + 1
    slots = reach * acc_blk
    here = lax.axis_index("ctx")
    pieces = [acceptor_feat]
    for offset in range(1, reach):
        pieces.append(
            passed_along(acceptor_feat, "ctx", -offset)
            if offset < blocks
            else jnp.zeros_like(acceptor_feat)
        )
    window = jnp.stack(pieces, axis=1).reshape(seq_dev, slots, width)
    pos_pad = jnp.concatenate(
        [acceptor_pos, jnp.zeros((seq_dev, SPAN_BLOCKS * acc_blk), jnp.int32)], axis=1
    )
    pos_win = lax.dynamic_slice_in_dim(pos_pad, here * acc_blk, slots, 1)
    slot_block = jnp.arange(slots, dtype=jnp.int32) // acc_blk
    inchain = here + slot_block < blocks
    dist = slot_block * BLOCK_BP + pos_win[:, None, :] - donor_pos[:, :, None]
    valid = (pair_mask > 0) & (dist > 0) & (dist <= SPAN_BLOCKS * BLOCK_BP) & inchain[None, None, :]
    bins = jnp.clip((dist - 1) // BIN_BP, 0, BINS - 1)
    lookup = (
        (bins[..., None] == jnp.arange(BINS, dtype=jnp.int32))
        .astype(jnp.bfloat16)
        .reshape(-1, BINS)
    )
    table = jnp.dot(lookup, dist_table, preferred_element_type=jnp.float32).reshape(
        seq_dev, don_blk, slots, width
    )
    pre = (
        donor_feat.astype(jnp.float32)[:, :, None, :] + window.astype(jnp.float32)[:, None] + table
    )
    flat = jax.nn.silu(pre).astype(jnp.bfloat16).reshape(-1, width)
    grad_pair = jnp.zeros((flat.shape[0], width), jnp.float32)
    losses = []
    fulls = []
    slot_ids = jnp.arange(slots, dtype=jnp.int32)
    for tissue in range(hidden_weights.shape[0]):
        w_in = hidden_weights[tissue]
        w_out = output_weights[tissue]
        goal = targets[:, :, tissue]
        hid = jnp.dot(flat, w_in, preferred_element_type=jnp.float32)
        act = jax.nn.silu(hid).astype(jnp.bfloat16)
        logits = jnp.dot(act, w_out, preferred_element_type=jnp.float32).reshape(
            seq_dev, don_blk, slots
        )
        masked = jnp.where(valid, logits, -jnp.inf)
        top = jnp.maximum(jnp.max(masked, axis=-1), 0.0)
        expo = jnp.exp(masked - top[..., None])
        total = jnp.sum(expo, axis=-1) + jnp.exp(-top)
        onehot = goal[..., None] == slot_ids
        picked = jnp.sum(jnp.where(onehot, logits, 0.0), axis=-1)
        losses.append(top + jnp.log(total) - picked)
        grad_logits = expo / total[..., None] - onehot.astype(jnp.float32)
        grad_act = grad_logits.reshape(-1)[:, None] * w_out.astype(jnp.float32)[None, :]
        grad_hid = (grad_act * silu_grad(hid)).astype(jnp.bfloat16)
        grad_pair = grad_pair + lax.dot_general(
            grad_hid, w_in, (((1,), (1,)), ((), ())), preferred_element_type=jnp.float32
        )
        fulls.append(
            lax.dot_general(
                flat, grad_hid, (((0,), (0,)), ((), ())), preferred_element_type=jnp.float32
            )
        )
    stacked = jnp.stack(fulls, axis=1)
    grad_hidden = jnp.transpose(
        lax.psum_scatter(stacked, ("ctx", "rep"), scatter_dimension=0, tiled=True), (1, 0, 2)
    )
    grad_pre = grad_pair.reshape(seq_dev, don_blk, slots, width) * silu_grad(pre)
    contrib = jnp.sum(grad_pre, axis=1).reshape(seq_dev, reach, acc_blk, width)
    carried = contrib[:, 0]
    for offset in range(1, min(reach, blocks)):
        carried = carried + passed_along(contrib[:, offset], "ctx", offset)
    grad_acceptor = lax.psum(carried, "tis")
    donor_loss = jnp.stack(losses, axis=-1)
    return (donor_loss, grad_hidden, grad_acceptor)


def silu_parts(values):
    sig = 0.5 * jnp.tanh(0.5 * values) + 0.5
    out = values * sig
    return out, sig + out * (1.0 - sig)


def spread(columns, lane):
    ids = lax.broadcasted_iota(jnp.int32, columns.shape, 1)
    return jnp.dot(
        jnp.where(ids == lane, columns, jnp.zeros_like(columns)),
        jnp.ones((LANES, LANES), jnp.bfloat16),
        preferred_element_type=jnp.float32,
    )


def head_kernel(blocks, don_blk, width, slots, *refs):
    packed = refs[:blocks]
    (apos_ref, table_ref, w_ref, wo_ref) = refs[blocks : blocks + 4]
    (gh_ref, acc_ref, loss_ref) = refs[blocks + 4 : blocks + 7]
    (feat, aux, pair_s, dpre_s, dhid_s, logit_s, gh_s) = refs[blocks + 7 :]
    here = lax.axis_index("ctx")
    rep = lax.axis_index("rep")
    cross = lax.div(rep, 2)
    core = lax.rem(rep, 2)
    blk = don_blk
    hidden = w_ref.shape[1]
    for k in range(blocks):
        owner = here ^ k
        feat[owner] = packed[k][:, : 2 * width].astype(jnp.float32)
        aux[owner] = packed[k][:, 2 * width :]
    ids = lax.broadcasted_iota(jnp.int32, (blk, LANES), 1)
    rows = lax.broadcasted_iota(jnp.int32, (blk, LANES), 0)
    w = w_ref[...]
    w_out = wo_ref[...].astype(jnp.float32)
    w_rep = jnp.broadcast_to(wo_ref[...], (LANES, hidden))
    table = table_ref[...]
    apos = apos_ref[...]
    ones = jnp.ones((LANES, LANES), jnp.bfloat16)

    def acceptor_rows(a):
        pos = jnp.zeros((blk, LANES), jnp.int32)
        wide = jnp.concatenate(
            [apos, jnp.zeros((1, LANES - apos.shape[1]), jnp.int32)], axis=1
        )
        wide = jnp.broadcast_to(wide, (blk, LANES))
        wide = jnp.where(ids == rows + a * blk, wide, pos)
        high = jnp.dot(
            (wide >> 8).astype(jnp.float32).astype(jnp.bfloat16), ones,
            preferred_element_type=jnp.float32,
        )
        low = jnp.dot(
            (wide & 255).astype(jnp.float32).astype(jnp.bfloat16), ones,
            preferred_element_type=jnp.float32,
        )
        return (high * 256.0 + low).astype(jnp.int32)

    apos_rows = [acceptor_rows(a) for a in range(blocks)]
    tile_of = {}
    for b in range(blocks):
        for a in range(b, min(blocks, b + SPAN_BLOCKS + 1)):
            tile_of[(b, a)] = len(tile_of)
    lane3 = lax.broadcasted_iota(jnp.int32, (blk, blk, LANES), 2)
    row3 = lax.broadcasted_iota(jnp.int32, (blk, blk, LANES), 1)
    acc_total = [jnp.zeros((blk, width), jnp.float32) for _ in range(blocks)]
    gh_total = None
    for b in range(blocks):
        extra = aux[b]
        dpos = (spread(extra, slots) * 256.0 + spread(extra, slots + 1)).astype(jnp.int32)
        goal = spread(extra, slots + 2 + here).astype(jnp.int32)
        donors = feat[b, :, :width]
        near = list(range(b, min(blocks, b + SPAN_BLOCKS + 1)))
        valids = []
        logits = []
        for a in near:
            k = a - b
            tile = tile_of[(b, a)]
            dist = k * BLOCK_BP + apos_rows[a][None] - dpos[:, None, :]
            open_slot = jnp.where(
                lane3 == row3 + k * blk, extra.astype(jnp.float32)[:, None, :], 0.0
            ).astype(jnp.bfloat16)
            mask = jnp.dot(
                open_slot.reshape(blk * blk, LANES), ones, preferred_element_type=jnp.float32
            ).reshape(blk, blk, LANES)
            valids.append((mask > 0.5) & (dist > 0) & (dist <= SPAN_BLOCKS * BLOCK_BP))
            bins = jnp.clip((dist - 1) >> 11, 0, BINS - 1)
            lookup = jnp.where(bins == lane3, 1.0, 0.0).astype(jnp.bfloat16)
            looked = jnp.dot(
                lookup.reshape(blk * blk, BINS), table, preferred_element_type=jnp.float32
            )
            pre = (donors[:, None, :] + feat[a, :, width:][None]).reshape(
                blk * blk, width
            ) + looked
            value, slope = silu_parts(pre)
            pair = value.astype(jnp.bfloat16)
            pair_s[tile] = pair
            dpre_s[tile] = slope
            hid = jnp.dot(pair, w, preferred_element_type=jnp.float32)
            value, slope = silu_parts(hid)
            dhid_s[tile] = slope * w_out
            logits.append(
                lax.dot_general(
                    value.astype(jnp.bfloat16),
                    w_rep,
                    (((1,), (1,)), ((), ())),
                    preferred_element_type=jnp.float32,
                ).reshape(blk, blk, LANES)
            )
        top = jnp.zeros((blk, 1, LANES), jnp.float32)
        for valid, logit in zip(valids, logits):
            top = jnp.maximum(
                top, jnp.max(jnp.where(valid, logit, -jnp.inf), axis=1, keepdims=True)
            )
        total = jnp.exp(-top)
        picked = jnp.zeros((blk, 1, LANES), jnp.float32)
        expos = []
        goals = []
        for a, valid, logit in zip(near, valids, logits):
            expo = jnp.exp(jnp.where(valid, logit, -jnp.inf) - top)
            total = total + jnp.sum(expo, axis=1, keepdims=True)
            chosen = goal[:, None, :] == row3 + (a - b) * blk
            picked = picked + jnp.sum(jnp.where(chosen, logit, 0.0), axis=1, keepdims=True)
            expos.append(expo)
            goals.append(chosen)
        loss_ref[b ^ here] = (top + jnp.log(total) - picked).reshape(blk, LANES)
        share = 1.0 / total
        for a, expo, chosen in zip(near, expos, goals):
            tile = tile_of[(b, a)]
            grad_logit = (expo * share - jnp.where(chosen, 1.0, 0.0)).reshape(blk * blk, LANES)
            grad_logit = jnp.concatenate([grad_logit] * (hidden // LANES), axis=1)
            grad_hid = (grad_logit * dhid_s[tile]).astype(jnp.bfloat16)
            part = lax.dot_general(
                pair_s[tile], grad_hid, (((0,), (0,)), ((), ())),
                preferred_element_type=jnp.float32,
            )
            if tile == 0:
                gh_s[...] = part
            else:
                gh_s[...] += part
            grad_pair = lax.dot_general(
                grad_hid, w, (((1,), (1,)), ((), ())), preferred_element_type=jnp.float32
            )
            acc_total[a] = acc_total[a] + jnp.sum(
                (grad_pair * dpre_s[tile]).reshape(blk, blk, width), axis=0
            )
    for a in range(blocks):
        acc_ref[a ^ here] = acc_total[a]
    chunk = gh_ref.shape[3]
    for c in range(blocks):
        for x in range(2):
            for y in range(2):
                start = ((c * 2 + x) * 2 + y) * chunk
                gh_ref[y ^ core, x ^ cross, c ^ here] = gh_s[start : start + chunk, :]


def finish_kernel(parts, width, hidden, *refs):
    pieces = refs[:parts]
    (loss_ref, gh_ref, acc_ref) = refs[parts:]
    here = lax.axis_index("ctx")
    total = None
    lanes = lax.broadcasted_iota(jnp.int32, (pieces[0].shape[0], LANES), 1)
    losses = jnp.zeros(lanes.shape, jnp.float32)
    for k in range(parts):
        owner = here ^ k
        gh_ref[owner] = pieces[k][:, :hidden]
        acc = pieces[k][:, hidden : hidden + width]
        total = acc if total is None else total + acc
        losses = jnp.where(lanes == owner, pieces[k][:, hidden + width :], losses)
    acc_ref[0] = total
    loss_ref[0] = losses[:, :parts]


def shared(
    donor_feat,
    acceptor_feat,
    donor_pos,
    acceptor_pos,
    pair_mask,
    targets,
    dist_table,
    hidden_weights,
    output_weights,
):
    _, blk, width = donor_feat.shape
    blocks = lax.axis_size("ctx")
    slots = pair_mask.shape[2]
    tissues, _, hidden = hidden_weights.shape
    here = lax.axis_index("ctx")
    bf16 = jnp.bfloat16
    spare = LANES - slots - 2 - tissues
    packed = jnp.concatenate(
        [
            donor_feat[0],
            acceptor_feat[0],
            pair_mask[0].astype(bf16),
            (donor_pos[0] >> 8).astype(bf16)[:, None],
            (donor_pos[0] & 255).astype(bf16)[:, None],
            targets[0].astype(bf16),
            jnp.zeros((blk, spare), bf16),
        ],
        axis=1,
    )
    pieces = [packed] + [swapped(packed, "ctx", k) for k in range(1, blocks)]
    w_in = lax.dynamic_index_in_dim(hidden_weights, here, 0, False)
    w_out = lax.dynamic_index_in_dim(output_weights, here, 0, True)
    tiles = sum(min(blocks, b + SPAN_BLOCKS + 1) - b for b in range(blocks))
    chunk = width // (4 * blocks)
    pairs = blk * blk
    partial, acc, loss = pl.pallas_call(
        functools.partial(head_kernel, blocks, blk, width, slots),
        out_shape=(
            jax.ShapeDtypeStruct((2, 2, blocks, chunk, hidden), jnp.float32),
            jax.ShapeDtypeStruct((blocks, blk, width), jnp.float32),
            jax.ShapeDtypeStruct((blocks, blk, LANES), jnp.float32),
        ),
        scratch_shapes=[
            pltpu.VMEM((blocks, blk, 2 * width), jnp.float32),
            pltpu.VMEM((blocks, blk, LANES), bf16),
            pltpu.VMEM((tiles, pairs, width), bf16),
            pltpu.VMEM((tiles, pairs, width), jnp.float32),
            pltpu.VMEM((tiles, pairs, hidden), jnp.float32),
            pltpu.VMEM((tiles, pairs, LANES), jnp.float32),
            pltpu.VMEM((width, hidden), jnp.float32),
        ],
        compiler_params=pltpu.CompilerParams(vmem_limit_bytes=48 * 2**20),
        name="head",
    )(*pieces, acceptor_pos, dist_table, w_in, w_out)
    acc = acc + swapped(acc, "tis", 1)
    partial = partial[0] + swapped(partial[1], "rep", 1)
    partial = partial[0] + swapped(partial[1].astype(bf16), "rep", 2).astype(jnp.float32)
    send = jnp.concatenate([partial, acc, loss], axis=2)
    arrived = [send[0]] + [swapped(send[k], "ctx", k) for k in range(1, blocks)]
    return pl.pallas_call(
        functools.partial(finish_kernel, blocks, width, hidden),
        out_shape=(
            jax.ShapeDtypeStruct((1, blk, tissues), jnp.float32),
            jax.ShapeDtypeStruct((tissues, chunk, hidden), jnp.float32),
            jax.ShapeDtypeStruct((1, blk, width), jnp.float32),
        ),
        name="finish",
    )(*arrived)


def on_device(*args):
    donor_feat, acceptor_feat, _, _, pair_mask, _, _, hidden_weights, _ = args
    blocks = lax.axis_size("ctx")
    tissues, width, hidden = hidden_weights.shape
    blk = donor_feat.shape[1]
    fits = (
        donor_feat.shape[0] == 1
        and tissues == blocks == 4
        and lax.axis_size("rep") == 4
        and lax.axis_size("tis") == 2
        and acceptor_feat.shape[1] == blk == 16
        and width == 256
        and hidden % LANES == 0
        and pair_mask.shape[2] + 2 + tissues <= LANES
    )
    return shared(*args) if fits else general(*args)


def solution(mesh):
    placed = (
        P("rep", "ctx", None),
        P("rep", "ctx", None),
        P("rep", "ctx"),
        P("rep", None),
        P("rep", "ctx", None),
        P("rep", "ctx", "tis"),
        P(),
        P("tis", None, None),
        P("tis", None),
    )
    return jax.shard_map(
        on_device,
        mesh=mesh,
        in_specs=placed,
        out_specs=(P("rep", "ctx", "tis"), P("tis", ("ctx", "rep"), None), P("rep", "ctx", None)),
        check_vma=False,
    )
```

```python
import functools

import jax
import jax.numpy as jnp
from jax import lax
from jax.experimental import pallas as pl
from jax.experimental.pallas import tpu as pltpu
from jax.sharding import PartitionSpec as P

BLOCK_BP = 65536
SPAN_BLOCKS = 4
BIN_BP = 2048
BINS = 128
LANES = 128


def passed_along(value, axis, steps):
    count = lax.axis_size(axis)
    first, last = (max(0, -steps), min(count, count - steps))
    return lax.ppermute(value, axis, [(source, source + steps) for source in range(first, last)])


def swapped(value, axis, bits):
    return lax.ppermute(value, axis, [(i, i ^ bits) for i in range(lax.axis_size(axis))])


def silu_grad(values):
    sig = jax.nn.sigmoid(values)
    return sig * (1.0 + values * (1.0 - sig))


def general(
    donor_feat,
    acceptor_feat,
    donor_pos,
    acceptor_pos,
    pair_mask,
    targets,
    dist_table,
    hidden_weights,
    output_weights,
):
    seq_dev, don_blk, width = donor_feat.shape
    acc_blk = acceptor_feat.shape[1]
    blocks = lax.axis_size("ctx")
    reach = SPAN_BLOCKS + 1
    slots = reach * acc_blk
    here = lax.axis_index("ctx")
    pieces = [acceptor_feat]
    for offset in range(1, reach):
        pieces.append(
            passed_along(acceptor_feat, "ctx", -offset)
            if offset < blocks
            else jnp.zeros_like(acceptor_feat)
        )
    window = jnp.stack(pieces, axis=1).reshape(seq_dev, slots, width)
    pos_pad = jnp.concatenate(
        [acceptor_pos, jnp.zeros((seq_dev, SPAN_BLOCKS * acc_blk), jnp.int32)], axis=1
    )
    pos_win = lax.dynamic_slice_in_dim(pos_pad, here * acc_blk, slots, 1)
    slot_block = jnp.arange(slots, dtype=jnp.int32) // acc_blk
    inchain = here + slot_block < blocks
    dist = slot_block * BLOCK_BP + pos_win[:, None, :] - donor_pos[:, :, None]
    valid = (pair_mask > 0) & (dist > 0) & (dist <= SPAN_BLOCKS * BLOCK_BP) & inchain[None, None, :]
    bins = jnp.clip((dist - 1) // BIN_BP, 0, BINS - 1)
    lookup = (
        (bins[..., None] == jnp.arange(BINS, dtype=jnp.int32))
        .astype(jnp.bfloat16)
        .reshape(-1, BINS)
    )
    table = jnp.dot(lookup, dist_table, preferred_element_type=jnp.float32).reshape(
        seq_dev, don_blk, slots, width
    )
    pre = (
        donor_feat.astype(jnp.float32)[:, :, None, :] + window.astype(jnp.float32)[:, None] + table
    )
    flat = jax.nn.silu(pre).astype(jnp.bfloat16).reshape(-1, width)
    grad_pair = jnp.zeros((flat.shape[0], width), jnp.float32)
    losses = []
    fulls = []
    slot_ids = jnp.arange(slots, dtype=jnp.int32)
    for tissue in range(hidden_weights.shape[0]):
        w_in = hidden_weights[tissue]
        w_out = output_weights[tissue]
        goal = targets[:, :, tissue]
        hid = jnp.dot(flat, w_in, preferred_element_type=jnp.float32)
        act = jax.nn.silu(hid).astype(jnp.bfloat16)
        logits = jnp.dot(act, w_out, preferred_element_type=jnp.float32).reshape(
            seq_dev, don_blk, slots
        )
        masked = jnp.where(valid, logits, -jnp.inf)
        top = jnp.maximum(jnp.max(masked, axis=-1), 0.0)
        expo = jnp.exp(masked - top[..., None])
        total = jnp.sum(expo, axis=-1) + jnp.exp(-top)
        onehot = goal[..., None] == slot_ids
        picked = jnp.sum(jnp.where(onehot, logits, 0.0), axis=-1)
        losses.append(top + jnp.log(total) - picked)
        grad_logits = expo / total[..., None] - onehot.astype(jnp.float32)
        grad_act = grad_logits.reshape(-1)[:, None] * w_out.astype(jnp.float32)[None, :]
        grad_hid = (grad_act * silu_grad(hid)).astype(jnp.bfloat16)
        grad_pair = grad_pair + lax.dot_general(
            grad_hid, w_in, (((1,), (1,)), ((), ())), preferred_element_type=jnp.float32
        )
        fulls.append(
            lax.dot_general(
                flat, grad_hid, (((0,), (0,)), ((), ())), preferred_element_type=jnp.float32
            )
        )
    stacked = jnp.stack(fulls, axis=1)
    grad_hidden = jnp.transpose(
        lax.psum_scatter(stacked, ("ctx", "rep"), scatter_dimension=0, tiled=True), (1, 0, 2)
    )
    grad_pre = grad_pair.reshape(seq_dev, don_blk, slots, width) * silu_grad(pre)
    contrib = jnp.sum(grad_pre, axis=1).reshape(seq_dev, reach, acc_blk, width)
    carried = contrib[:, 0]
    for offset in range(1, min(reach, blocks)):
        carried = carried + passed_along(contrib[:, offset], "ctx", offset)
    grad_acceptor = lax.psum(carried, "tis")
    donor_loss = jnp.stack(losses, axis=-1)
    return (donor_loss, grad_hidden, grad_acceptor)


def halved(value):
    return (value.astype(jnp.float32) * 0.5).astype(value.dtype)


def silu_parts(half):
    turn = jnp.tanh(half)
    tilted = half * turn
    return half + tilted, (1.0 + turn) * ((1.0 + half) - tilted)


def ones_dot(left, right):
    return jnp.dot(left, right, preferred_element_type=jnp.float32)


def tiles_of(blocks):
    return [(b, a) for b in range(blocks) for a in range(b, min(blocks, b + SPAN_BLOCKS + 1))]


def head_kernel(blocks, blk, width, *refs):
    packed = refs[:blocks]
    (table_ref, w_ref, wo_ref) = refs[blocks : blocks + 3]
    (gh_ref, loss_ref, grad_s, dpre_s) = refs[blocks + 3 : blocks + 7]
    (source, aux, picks_s, pair_s, act_s, dhid_s, gh_s) = refs[blocks + 7 :]
    here = lax.axis_index("ctx")
    rep = lax.axis_index("rep")
    cross = lax.div(rep, 2)
    core = lax.rem(rep, 2)
    f32, bf16 = jnp.float32, jnp.bfloat16
    hidden = w_ref.shape[1]
    pairs = blk * blk
    sites = blocks * blk
    tiles = tiles_of(blocks)

    source[:BINS, :] = table_ref[...]
    for k in range(blocks):
        start = pl.multiple_of((here ^ k) * blk, blk)
        piece = packed[k][...].astype(bf16)
        source[pl.ds(BINS + start, blk), :] = halved(piece[:, :width])
        source[pl.ds(BINS + sites + start, blk), :] = halved(piece[:, width : 2 * width])
        aux[pl.ds(start, blk), :] = piece[:, 2 * width :]

    w_half = w_ref[...]
    w_out = wo_ref[...]
    w_rows = jnp.broadcast_to(w_out, (LANES, hidden)).astype(bf16)
    w_out = w_out * 0.5
    ones = jnp.ones((LANES, LANES), bf16)
    lane3 = lax.broadcasted_iota(jnp.int32, (blk, blk, LANES), 2)
    row3 = lax.broadcasted_iota(jnp.int32, (blk, blk, LANES), 1)
    don3 = lax.broadcasted_iota(jnp.int32, (blk, blk, LANES), 0)
    lane_f = lax.broadcasted_iota(jnp.int32, (pairs, LANES), 1).astype(f32)
    from_donor = [
        jnp.where(lane3 == don3 + b * blk, 1.0, 0.0).astype(bf16).reshape(pairs, LANES)
        for b in range(blocks)
    ]
    from_acceptor = [
        jnp.where(lane3 == row3 + (sites + a * blk), 1.0, 0.0).astype(bf16).reshape(pairs, LANES)
        for a in range(blocks)
    ]
    slot_of = [lane3 == row3 + a * blk for a in range(blocks)]
    twice_of = [pick | (lane3 == row3 + (sites + a * blk)) for a, pick in enumerate(slot_of)]
    lanes = lax.broadcasted_iota(jnp.int32, (blk, LANES), 1)
    codes = [aux[b * blk : (b + 1) * blk, :].astype(f32) for b in range(blocks)]
    for tile, (b, a) in enumerate(tiles):
        code = jnp.where(slot_of[a], codes[b][:, None, :], 0.0).astype(bf16)
        code = ones_dot(code.reshape(pairs, LANES), ones)
        picks_s[tile] = jnp.where(code == lane_f, 1.0, 0.0).astype(bf16)
    for tile, (b, a) in enumerate(tiles):
        picks = jnp.concatenate([picks_s[tile], from_donor[b] + from_acceptor[a]], axis=1)
        value, slope = silu_parts(ones_dot(picks, source[...]))
        pair_s[tile] = value.astype(bf16)
        dpre_s[tile] = slope
    for tile in range(len(tiles)):
        value, slope = silu_parts(ones_dot(pair_s[tile], w_half))
        act_s[tile] = value.astype(bf16)
        dhid_s[tile] = slope * w_out
    spread_out = [jnp.zeros((blk, blk, LANES), f32)] * blocks
    for tile, (b, a) in enumerate(tiles):
        logit = lax.dot_general(
            act_s[tile], w_rows, (((1,), (1,)), ((), ())), preferred_element_type=f32
        )
        spread_out[b] = jnp.where(slot_of[a], logit.reshape(blk, blk, LANES), spread_out[b])
    grads = []
    for b in range(blocks):
        logit = jnp.sum(spread_out[b], axis=1)
        valid = (codes[b] >= 0.0) & (lanes < sites)
        goal = jnp.sum(jnp.where(lanes == sites + here, codes[b], 0.0), axis=1, keepdims=True)
        chosen = lanes == goal.astype(jnp.int32)
        masked = jnp.where(valid, logit, -jnp.inf)
        top = jnp.maximum(jnp.max(masked, axis=1, keepdims=True), 0.0)
        expo = jnp.exp(masked - top)
        total = jnp.sum(expo, axis=1, keepdims=True) + jnp.exp(-top)
        picked = jnp.sum(jnp.where(chosen, logit, 0.0), axis=1, keepdims=True)
        loss_ref[b ^ here] = jnp.broadcast_to(top + jnp.log(total) - picked, (blk, LANES))
        grad = expo / total - jnp.where(chosen, 1.0, 0.0)
        high = grad.astype(bf16).astype(f32)
        grads.append(high + pltpu.roll(grad - high, sites, 1))
    for tile, (b, a) in enumerate(tiles):
        rows = jnp.where(twice_of[a], grads[b][:, None, :], 0.0).astype(bf16)
        rows = ones_dot(rows.reshape(pairs, LANES), ones)
        rows = jnp.concatenate([rows] * (hidden // LANES), axis=1)
        grad_s[tile] = (rows * dhid_s[tile]).astype(bf16)
    count = len(tiles) * pairs
    gh_s[...] = lax.dot_general(
        pair_s[...].reshape(count, width),
        grad_s[...].reshape(count, hidden),
        (((0,), (0,)), ((), ())),
        preferred_element_type=f32,
    )
    chunk = gh_ref.shape[3]
    for c in range(blocks):
        for x in range(2):
            for y in range(2):
                start = ((c * 2 + x) * 2 + y) * chunk
                gh_ref[y ^ core, x ^ cross, c ^ here] = gh_s[start : start + chunk, :]


def finish_kernel(parts, width, hidden, *refs):
    pieces = refs[:parts]
    (loss_ref, gh_ref, acc_ref) = refs[parts:]
    here = lax.axis_index("ctx")
    blk = pieces[0].shape[0]
    total = None
    diagonal = lax.broadcasted_iota(jnp.int32, (blk, LANES), 0) == lax.broadcasted_iota(
        jnp.int32, (blk, LANES), 1
    )
    for k in range(parts):
        owner = here ^ k
        gh_ref[owner] = pieces[k][:, :hidden]
        acc = pieces[k][:, hidden : hidden + width]
        total = acc if total is None else total + acc
        row = jnp.sum(
            jnp.where(diagonal, pieces[k][:, hidden + width :], 0.0), axis=0, keepdims=True
        )
        loss_ref[0, pl.ds(owner, 1), :] = row[:, :blk]
    acc_ref[0] = total


def pack_kernel(
    blocks, pos_ref, goal_ref, apos_ref, donor_hbm, acceptor_hbm, mask_hbm, out_ref, mask_ref, sems
):
    here = lax.axis_index("ctx")
    f32, bf16 = jnp.float32, jnp.bfloat16
    _, blk, width = donor_hbm.shape
    copies = [
        pltpu.make_async_copy(mask_hbm, mask_ref, sems.at[0]),
        pltpu.make_async_copy(donor_hbm.at[0], out_ref.at[:, :width], sems.at[1]),
        pltpu.make_async_copy(acceptor_hbm.at[0], out_ref.at[:, width : 2 * width], sems.at[2]),
    ]
    for copy in copies:
        copy.start()
    tissues = goal_ref.shape[1]
    slots = mask_ref.shape[2]
    sites = blocks * blk
    lanes = lax.broadcasted_iota(jnp.int32, (blk, LANES), 1)
    rows = lax.broadcasted_iota(jnp.int32, (blk, LANES), 0)
    dpos = jnp.zeros((blk, LANES), jnp.int32)
    goal = jnp.zeros((blk, LANES), jnp.int32)
    for i in range(blk):
        dpos = jnp.where(rows == i, pos_ref[0, i], dpos)
        for t in range(tissues):
            goal = jnp.where((rows == i) & (lanes == sites + t), goal_ref[0, t, i], goal)
    apos = jnp.zeros((1, LANES), jnp.int32)
    line = lax.broadcasted_iota(jnp.int32, (1, LANES), 1)
    for j in range(sites):
        apos = jnp.where(line == j, apos_ref[0, j], apos)
    dist = (lanes // blk - here) * BLOCK_BP + apos - dpos
    goal = jnp.where(goal == slots, -1, goal + here * blk)
    spot = lax.broadcasted_iota(jnp.int32, (LANES, LANES), 0)
    onto = lax.broadcasted_iota(jnp.int32, (LANES, LANES), 1)
    shift = jnp.where((onto == spot + here * blk) & (spot < slots), 1.0, 0.0).astype(bf16)
    copies[0].wait()
    mask = jnp.concatenate(
        [mask_ref[0], jnp.zeros((blk, LANES - slots), jnp.int32)], axis=1
    )
    mask = ones_dot(mask.astype(f32).astype(bf16), shift)
    valid = (mask > 0.5) & (dist > 0) & (dist <= SPAN_BLOCKS * BLOCK_BP) & (lanes < sites)
    code = jnp.where(valid, jnp.clip((dist - 1) // BIN_BP, 0, BINS - 1), -1)
    code = jnp.where(lanes < sites, code, goal)
    out_ref[:, 2 * width :] = code.astype(f32).astype(bf16)
    copies[1].wait()
    copies[2].wait()


def acceptor_kernel(blocks, blk, grad_ref, w_ref, slope_ref, out_ref):
    here = lax.axis_index("ctx")
    width = w_ref.shape[0]
    w = w_ref[...]
    total = [None] * blocks
    for tile, (_, a) in enumerate(tiles_of(blocks)):
        grad_pair = lax.dot_general(
            grad_ref[tile], w, (((1,), (1,)), ((), ())), preferred_element_type=jnp.float32
        )
        part = jnp.sum((grad_pair * slope_ref[tile]).reshape(blk, blk, width), axis=0)
        total[a] = part if total[a] is None else total[a] + part
    for a in range(blocks):
        out_ref[a ^ here] = total[a]


def shared(
    donor_feat,
    acceptor_feat,
    donor_pos,
    acceptor_pos,
    pair_mask,
    targets,
    dist_table,
    hidden_weights,
    output_weights,
):
    _, blk, width = donor_feat.shape
    blocks = lax.axis_size("ctx")
    tissues, _, hidden = hidden_weights.shape
    bf16 = jnp.bfloat16
    f32 = jnp.float32
    anywhere = pl.BlockSpec(memory_space=pl.ANY)
    smem = pl.BlockSpec(memory_space=pltpu.SMEM)
    packed = pl.pallas_call(
        functools.partial(pack_kernel, blocks),
        in_specs=[smem] * 3 + [anywhere] * 3,
        out_specs=pl.BlockSpec(memory_space=pltpu.VMEM),
        out_shape=jax.ShapeDtypeStruct((blk, 2 * width + LANES), bf16),
        scratch_shapes=[
            pltpu.VMEM(pair_mask.shape, jnp.int32),
            pltpu.SemaphoreType.DMA((3,)),
        ],
        compiler_params=pltpu.CompilerParams(vmem_limit_bytes=60 * 2**20),
        name="pack",
    )(
        donor_pos,
        jnp.transpose(targets, (0, 2, 1)),
        acceptor_pos,
        donor_feat,
        acceptor_feat,
        pair_mask,
    )
    here = lax.axis_index("ctx")
    table = halved(dist_table)
    w_in = halved(lax.dynamic_index_in_dim(hidden_weights, here, 0, False))
    w_out = lax.dynamic_index_in_dim(output_weights, here, 0, True).astype(f32)
    pieces = [packed.astype(f32)] + [swapped(packed, "ctx", k) for k in range(1, blocks)]
    tiles = len(tiles_of(blocks))
    chunk = width // (4 * blocks)
    pairs = blk * blk
    partial, loss, grad, slope = pl.pallas_call(
        functools.partial(head_kernel, blocks, blk, width),
        out_shape=(
            jax.ShapeDtypeStruct((2, 2, blocks, chunk, hidden), f32),
            jax.ShapeDtypeStruct((blocks, blk, LANES), f32),
            jax.ShapeDtypeStruct((tiles, pairs, hidden), bf16),
            jax.ShapeDtypeStruct((tiles, pairs, width), f32),
        ),
        scratch_shapes=[
            pltpu.VMEM((BINS + 2 * blocks * blk, width), bf16),
            pltpu.VMEM((blocks * blk, LANES), bf16),
            pltpu.VMEM((tiles, pairs, BINS), bf16),
            pltpu.VMEM((tiles, pairs, width), bf16),
            pltpu.VMEM((tiles, pairs, hidden), bf16),
            pltpu.VMEM((tiles, pairs, hidden), f32),
            pltpu.VMEM((width, hidden), f32),
        ],
        compiler_params=pltpu.CompilerParams(vmem_limit_bytes=32 * 2**20),
        name="head",
    )(*pieces, table, w_in, w_out)
    kept, sent = partial[0], swapped(partial[1], "rep", 1)
    acc = pl.pallas_call(
        functools.partial(acceptor_kernel, blocks, blk),
        out_shape=jax.ShapeDtypeStruct((blocks, blk, width), f32),
        compiler_params=pltpu.CompilerParams(vmem_limit_bytes=16 * 2**20),
        cost_estimate=pl.CostEstimate(
            flops=2 * tiles * pairs * width * hidden,
            bytes_accessed=tiles * pairs * (2 * hidden + 4 * width),
            transcendentals=0,
        ),
        name="acceptors",
    )(grad, w_in, slope)
    partial = kept + sent
    sent = swapped(partial[1].astype(bf16), "rep", 2)
    acc = acc + swapped(acc, "tis", 1)
    partial = partial[0] + sent.astype(jnp.float32)
    send = jnp.concatenate([partial, acc, loss], axis=2)
    arrived = [send[0]] + [swapped(send[k], "ctx", k) for k in range(1, blocks)]
    donor_loss, grad_hidden, grad_acceptor = pl.pallas_call(
        functools.partial(finish_kernel, blocks, width, hidden),
        out_shape=(
            jax.ShapeDtypeStruct((1, tissues, blk), jnp.float32),
            jax.ShapeDtypeStruct((tissues, chunk, hidden), jnp.float32),
            jax.ShapeDtypeStruct((1, blk, width), jnp.float32),
        ),
        compiler_params=pltpu.CompilerParams(vmem_limit_bytes=8 * 2**20),
        name="finish",
    )(*arrived)
    return (jnp.transpose(donor_loss, (0, 2, 1)), grad_hidden, grad_acceptor)


def on_device(*args):
    donor_feat, acceptor_feat, _, _, pair_mask, _, _, hidden_weights, _ = args
    blocks = lax.axis_size("ctx")
    tissues, width, hidden = hidden_weights.shape
    blk = donor_feat.shape[1]
    fits = (
        donor_feat.shape[0] == 1
        and tissues == blocks == 4
        and lax.axis_size("rep") == 4
        and lax.axis_size("tis") == 2
        and acceptor_feat.shape[1] == blk == 16
        and width == 256
        and hidden % LANES == 0
        and pair_mask.shape[2] == (SPAN_BLOCKS + 1) * blk
        and BINS == LANES == 2 * blocks * blk
    )
    return shared(*args) if fits else general(*args)


def solution(mesh):
    placed = (
        P("rep", "ctx", None),
        P("rep", "ctx", None),
        P("rep", "ctx"),
        P("rep", None),
        P("rep", "ctx", None),
        P("rep", "ctx", "tis"),
        P(),
        P("tis", None, None),
        P("tis", None),
    )
    return jax.shard_map(
        on_device,
        mesh=mesh,
        in_specs=placed,
        out_specs=(P("rep", "ctx", "tis"), P("tis", ("ctx", "rep"), None), P("rep", "ctx", None)),
        check_vma=False,
    )
```

```python
import functools

import jax
import jax.numpy as jnp
from jax import lax
from jax.experimental import pallas as pl
from jax.experimental.pallas import tpu as pltpu
from jax.sharding import PartitionSpec as P

BLOCK_BP = 65536
SPAN_BLOCKS = 4
BIN_BP = 2048
BINS = 128
LANES = 128
GATHER_ORDER = (1, 3, 2)
RETURN_ORDER = (1, 3, 2)
LAGS = (10, 12, 13)


def passed_along(value, axis, steps):
    count = lax.axis_size(axis)
    first, last = (max(0, -steps), min(count, count - steps))
    return lax.ppermute(value, axis, [(source, source + steps) for source in range(first, last)])


def swapped(value, axis, bits):
    return lax.ppermute(value, axis, [(i, i ^ bits) for i in range(lax.axis_size(axis))])


def silu_grad(values):
    sig = jax.nn.sigmoid(values)
    return sig * (1.0 + values * (1.0 - sig))


def general(
    donor_feat,
    acceptor_feat,
    donor_pos,
    acceptor_pos,
    pair_mask,
    targets,
    dist_table,
    hidden_weights,
    output_weights,
):
    seq_dev, don_blk, width = donor_feat.shape
    acc_blk = acceptor_feat.shape[1]
    blocks = lax.axis_size("ctx")
    reach = SPAN_BLOCKS + 1
    slots = reach * acc_blk
    here = lax.axis_index("ctx")
    pieces = [acceptor_feat]
    for offset in range(1, reach):
        pieces.append(
            passed_along(acceptor_feat, "ctx", -offset)
            if offset < blocks
            else jnp.zeros_like(acceptor_feat)
        )
    window = jnp.stack(pieces, axis=1).reshape(seq_dev, slots, width)
    pos_pad = jnp.concatenate(
        [acceptor_pos, jnp.zeros((seq_dev, SPAN_BLOCKS * acc_blk), jnp.int32)], axis=1
    )
    pos_win = lax.dynamic_slice_in_dim(pos_pad, here * acc_blk, slots, 1)
    slot_block = jnp.arange(slots, dtype=jnp.int32) // acc_blk
    inchain = here + slot_block < blocks
    dist = slot_block * BLOCK_BP + pos_win[:, None, :] - donor_pos[:, :, None]
    valid = (pair_mask > 0) & (dist > 0) & (dist <= SPAN_BLOCKS * BLOCK_BP) & inchain[None, None, :]
    bins = jnp.clip((dist - 1) // BIN_BP, 0, BINS - 1)
    lookup = (
        (bins[..., None] == jnp.arange(BINS, dtype=jnp.int32))
        .astype(jnp.bfloat16)
        .reshape(-1, BINS)
    )
    table = jnp.dot(lookup, dist_table, preferred_element_type=jnp.float32).reshape(
        seq_dev, don_blk, slots, width
    )
    pre = (
        donor_feat.astype(jnp.float32)[:, :, None, :] + window.astype(jnp.float32)[:, None] + table
    )
    flat = jax.nn.silu(pre).astype(jnp.bfloat16).reshape(-1, width)
    grad_pair = jnp.zeros((flat.shape[0], width), jnp.float32)
    losses = []
    fulls = []
    slot_ids = jnp.arange(slots, dtype=jnp.int32)
    for tissue in range(hidden_weights.shape[0]):
        w_in = hidden_weights[tissue]
        w_out = output_weights[tissue]
        goal = targets[:, :, tissue]
        hid = jnp.dot(flat, w_in, preferred_element_type=jnp.float32)
        act = jax.nn.silu(hid).astype(jnp.bfloat16)
        logits = jnp.dot(act, w_out, preferred_element_type=jnp.float32).reshape(
            seq_dev, don_blk, slots
        )
        masked = jnp.where(valid, logits, -jnp.inf)
        top = jnp.maximum(jnp.max(masked, axis=-1), 0.0)
        expo = jnp.exp(masked - top[..., None])
        total = jnp.sum(expo, axis=-1) + jnp.exp(-top)
        onehot = goal[..., None] == slot_ids
        picked = jnp.sum(jnp.where(onehot, logits, 0.0), axis=-1)
        losses.append(top + jnp.log(total) - picked)
        grad_logits = expo / total[..., None] - onehot.astype(jnp.float32)
        grad_act = grad_logits.reshape(-1)[:, None] * w_out.astype(jnp.float32)[None, :]
        grad_hid = (grad_act * silu_grad(hid)).astype(jnp.bfloat16)
        grad_pair = grad_pair + lax.dot_general(
            grad_hid, w_in, (((1,), (1,)), ((), ())), preferred_element_type=jnp.float32
        )
        fulls.append(
            lax.dot_general(
                flat, grad_hid, (((0,), (0,)), ((), ())), preferred_element_type=jnp.float32
            )
        )
    stacked = jnp.stack(fulls, axis=1)
    grad_hidden = jnp.transpose(
        lax.psum_scatter(stacked, ("ctx", "rep"), scatter_dimension=0, tiled=True), (1, 0, 2)
    )
    grad_pre = grad_pair.reshape(seq_dev, don_blk, slots, width) * silu_grad(pre)
    contrib = jnp.sum(grad_pre, axis=1).reshape(seq_dev, reach, acc_blk, width)
    carried = contrib[:, 0]
    for offset in range(1, min(reach, blocks)):
        carried = carried + passed_along(contrib[:, offset], "ctx", offset)
    grad_acceptor = lax.psum(carried, "tis")
    donor_loss = jnp.stack(losses, axis=-1)
    return (donor_loss, grad_hidden, grad_acceptor)


def halved(value):
    return (value.astype(jnp.float32) * 0.5).astype(value.dtype)


def silu_parts(half):
    turn = jnp.tanh(half)
    tilted = half * turn
    return half + tilted, (1.0 + turn) * ((1.0 + half) - tilted)


def ones_dot(left, right):
    return jnp.dot(left, right, preferred_element_type=jnp.float32)


def tiles_of(blocks):
    return [(b, a) for b in range(blocks) for a in range(b, min(blocks, b + SPAN_BLOCKS + 1))]


def head_kernel(blocks, blk, width, *refs):
    (base_ref, w_ref) = refs[:2]
    packed = refs[2 : blocks + 1]
    (gh_ref, loss_ref, grad_s, dpre_s) = refs[blocks + 1 : blocks + 5]
    (source, aux, picks_s, pair_s, act_s, dhid_s, gh_s) = refs[blocks + 5 :]
    here = lax.axis_index("ctx")
    rep = lax.axis_index("rep")
    cross = lax.div(rep, 2)
    core = lax.rem(rep, 2)
    f32, bf16 = jnp.float32, jnp.bfloat16
    hidden = gh_s.shape[1]
    pairs = blk * blk
    sites = blocks * blk
    tiles = tiles_of(blocks)
    parts = hidden // width

    source[:BINS, :] = base_ref[:BINS, :]
    for i, k in enumerate((0,) + GATHER_ORDER):
        start = pl.multiple_of((here ^ k) * blk, blk)
        if k == 0:
            donors = base_ref[BINS : BINS + blk, :]
            acceptors = base_ref[BINS + blk : BINS + 2 * blk, :]
            codes = base_ref[BINS + 2 * blk : BINS + 3 * blk, :LANES]
            codes = (codes.astype(f32) * 2.0).astype(bf16)
        else:
            donors = halved(packed[i - 1][:, :width])
            acceptors = halved(packed[i - 1][:, width : 2 * width])
            codes = packed[i - 1][:, 2 * width :]
        source[pl.ds(BINS + start, blk), :] = donors
        source[pl.ds(BINS + sites + start, blk), :] = acceptors
        aux[pl.ds(start, blk), :] = codes

    w_half = w_ref[...]
    w_out = base_ref[BINS + 3 * blk : BINS + 4 * blk, :].astype(f32)
    w_out = jnp.concatenate([w_out[p : p + 1, :] for p in range(parts)], axis=1)
    w_rows = jnp.broadcast_to(w_out * 2.0, (LANES, hidden)).astype(bf16)
    ones = jnp.ones((LANES, LANES), bf16)
    lane3 = lax.broadcasted_iota(jnp.int32, (blk, blk, LANES), 2)
    row3 = lax.broadcasted_iota(jnp.int32, (blk, blk, LANES), 1)
    don3 = lax.broadcasted_iota(jnp.int32, (blk, blk, LANES), 0)
    lane_f = lax.broadcasted_iota(jnp.int32, (pairs, LANES), 1).astype(f32)
    from_donor = [
        jnp.where(lane3 == don3 + b * blk, 1.0, 0.0).astype(bf16).reshape(pairs, LANES)
        for b in range(blocks)
    ]
    from_acceptor = [
        jnp.where(lane3 == row3 + (sites + a * blk), 1.0, 0.0).astype(bf16).reshape(pairs, LANES)
        for a in range(blocks)
    ]
    slot_of = [lane3 == row3 + a * blk for a in range(blocks)]
    twice_of = [pick | (lane3 == row3 + (sites + a * blk)) for a, pick in enumerate(slot_of)]
    lanes = lax.broadcasted_iota(jnp.int32, (blk, LANES), 1)
    codes = [aux[b * blk : (b + 1) * blk, :].astype(f32) for b in range(blocks)]
    spread_out = [jnp.zeros((blk, blk, LANES), f32)] * blocks

    def bins_of(tile):
        b, a = tiles[tile]
        code = jnp.where(slot_of[a], codes[b][:, None, :], 0.0).astype(bf16)
        code = ones_dot(code.reshape(pairs, LANES), ones)
        picks_s[tile] = jnp.where(code == lane_f, 1.0, 0.0).astype(bf16)

    def pair_of(tile):
        b, a = tiles[tile]
        picks = jnp.concatenate([picks_s[tile], from_donor[b] + from_acceptor[a]], axis=1)
        value, slope = silu_parts(ones_dot(picks, source[...]))
        pair_s[tile] = value.astype(bf16)
        dpre_s[tile] = slope

    def hidden_of(tile):
        value, slope = silu_parts(ones_dot(pair_s[tile], w_half))
        act_s[tile] = value.astype(bf16)
        dhid_s[tile] = slope * w_out

    def logits_of(tile):
        b, a = tiles[tile]
        logit = lax.dot_general(
            act_s[tile], w_rows, (((1,), (1,)), ((), ())), preferred_element_type=f32
        )
        spread_out[b] = jnp.where(slot_of[a], logit.reshape(blk, blk, LANES), spread_out[b])

    stages = [(bins_of, 0), (pair_of, LAGS[0]), (hidden_of, LAGS[1]), (logits_of, LAGS[2])]
    for step in range(len(tiles) + stages[-1][1]):
        for stage, lag in stages:
            if 0 <= step - lag < len(tiles):
                stage(step - lag)
    grads = []
    for b in range(blocks):
        logit = jnp.sum(spread_out[b], axis=1)
        valid = (codes[b] >= 0.0) & (lanes < sites)
        goal = jnp.sum(jnp.where(lanes == sites + here, codes[b], 0.0), axis=1, keepdims=True)
        chosen = lanes == goal.astype(jnp.int32)
        masked = jnp.where(valid, logit, -jnp.inf)
        top = jnp.maximum(jnp.max(masked, axis=1, keepdims=True), 0.0)
        expo = jnp.exp(masked - top)
        total = jnp.sum(expo, axis=1, keepdims=True) + jnp.exp(-top)
        picked = jnp.sum(jnp.where(chosen, logit, 0.0), axis=1, keepdims=True)
        loss_ref[b ^ here] = jnp.broadcast_to(top + jnp.log(total) - picked, (blk, LANES))
        grad = expo / total - jnp.where(chosen, 1.0, 0.0)
        high = grad.astype(bf16).astype(f32)
        grads.append(high + pltpu.roll(grad - high, sites, 1))
    def gradient_of(start, stop):
        count = (stop - start) * pairs
        return lax.dot_general(
            pair_s[start:stop].reshape(count, width),
            grad_s[start:stop].reshape(count, hidden),
            (((0,), (0,)), ((), ())),
            preferred_element_type=f32,
        )

    middle = len(tiles) // 2
    for tile, (b, a) in enumerate(tiles):
        rows = jnp.where(twice_of[a], grads[b][:, None, :], 0.0).astype(bf16)
        rows = ones_dot(rows.reshape(pairs, LANES), ones)
        rows = jnp.concatenate([rows] * (hidden // LANES), axis=1)
        grad_s[tile] = (rows * dhid_s[tile]).astype(bf16)
        if tile == middle:
            gh_s[...] = gradient_of(0, middle)
    total = gh_s[...] + gradient_of(middle, len(tiles))
    chunk = gh_ref.shape[3]
    for c in range(blocks):
        for x in range(2):
            for y in range(2):
                start = ((c * 2 + x) * 2 + y) * chunk
                gh_ref[y ^ core, x ^ cross, c ^ here] = total[start : start + chunk, :]


def finish_kernel(parts, width, hidden, *refs):
    pieces = refs[:parts]
    (loss_ref, gh_ref, acc_ref) = refs[parts:]
    here = lax.axis_index("ctx")
    blk = pieces[0].shape[0]
    total = None
    diagonal = lax.broadcasted_iota(jnp.int32, (blk, LANES), 0) == lax.broadcasted_iota(
        jnp.int32, (blk, LANES), 1
    )
    for piece, k in zip(pieces, (0,) + RETURN_ORDER):
        owner = here ^ k
        gh_ref[owner] = piece[:, :hidden]
        acc = piece[:, hidden : hidden + width]
        total = acc if total is None else total + acc
        row = jnp.sum(
            jnp.where(diagonal, piece[:, hidden + width :], 0.0), axis=0, keepdims=True
        )
        loss_ref[0, pl.ds(owner, 1), :] = row[:, :blk]
    acc_ref[0] = total


def pack_kernel(
    blocks,
    pos_hbm,
    goal_hbm,
    apos_hbm,
    mask_hbm,
    donor_hbm,
    acceptor_hbm,
    wo_hbm,
    table_hbm,
    out_hbm,
    base_hbm,
    pos_ref,
    goal_ref,
    apos_ref,
    mask_ref,
    wo_ref,
    aux_ref,
    base_ref,
    sems,
):
    here = lax.axis_index("ctx")
    f32, bf16 = jnp.float32, jnp.bfloat16
    _, blk, width = donor_hbm.shape
    loads = [
        (donor_hbm.at[0], base_ref.at[BINS : BINS + blk]),
        (acceptor_hbm.at[0], base_ref.at[BINS + blk : BINS + 2 * blk]),
        (mask_hbm, mask_ref),
        (pos_hbm, pos_ref),
        (goal_hbm, goal_ref),
        (apos_hbm, apos_ref),
        (wo_hbm, wo_ref),
        (table_hbm, base_ref.at[:BINS]),
    ]
    stores = [
        (base_ref.at[BINS : BINS + blk], out_hbm.at[:, :width]),
        (base_ref.at[BINS + blk : BINS + 2 * blk], out_hbm.at[:, width : 2 * width]),
        (aux_ref, out_hbm.at[:, 2 * width :]),
        (base_ref, base_hbm),
    ]
    copies = [
        pltpu.make_async_copy(src, dst, sems.at[i]) for i, (src, dst) in enumerate(loads + stores)
    ]
    stores = copies[len(loads) :]
    loads = copies[: len(loads)]
    for copy in loads:
        copy.start()
    tissues = goal_ref.shape[1]
    slots = mask_ref.shape[2]
    sites = blocks * blk
    lanes = lax.broadcasted_iota(jnp.int32, (blk, LANES), 1)
    rows = lax.broadcasted_iota(jnp.int32, (blk, LANES), 0)
    spot = lax.broadcasted_iota(jnp.int32, (LANES, LANES), 0)
    onto = lax.broadcasted_iota(jnp.int32, (LANES, LANES), 1)
    shift = jnp.where((onto == spot + here * blk) & (spot < slots), 1.0, 0.0).astype(bf16)
    dpos = jnp.zeros((blk, LANES), jnp.int32)
    goal = jnp.zeros((blk, LANES), jnp.int32)
    for copy in loads:
        copy.wait()
    for copy in stores[:2]:
        copy.start()
    for i in range(blk):
        dpos = jnp.where(rows == i, pos_ref[0, i], dpos)
        for t in range(tissues):
            goal = jnp.where((rows == i) & (lanes == sites + t), goal_ref[0, t, i], goal)
    apos = jnp.zeros((1, LANES), jnp.int32)
    line = lax.broadcasted_iota(jnp.int32, (1, LANES), 1)
    for j in range(sites):
        apos = jnp.where(line == j, apos_ref[0, j], apos)
    dist = (lanes // blk - here) * BLOCK_BP + apos - dpos
    goal = jnp.where(goal == slots, -1, goal + here * blk)
    mask = jnp.concatenate(
        [mask_ref[0], jnp.zeros((blk, LANES - slots), jnp.int32)], axis=1
    )
    mask = ones_dot(mask.astype(f32).astype(bf16), shift)
    valid = (mask > 0.5) & (dist > 0) & (dist <= SPAN_BLOCKS * BLOCK_BP) & (lanes < sites)
    code = jnp.where(valid, jnp.clip((dist - 1) // BIN_BP, 0, BINS - 1), -1)
    code = jnp.where(lanes < sites, code, goal)
    code = code.astype(f32).astype(bf16)
    aux_ref[...] = code
    stores[2].start()
    wo_all = wo_ref[...].astype(f32)
    pick = lax.broadcasted_iota(jnp.int32, wo_all.shape, 0) == here
    row = jnp.sum(jnp.where(pick, wo_all, 0.0), axis=0, keepdims=True)
    start = BINS + 2 * blk
    base_ref[start : start + blk, :LANES] = code
    base_ref[start : start + blk, LANES:] = jnp.zeros((blk, width - LANES), bf16)
    parts = [row[:, i * width : (i + 1) * width] for i in range(row.shape[1] // width)]
    ids = lax.broadcasted_iota(jnp.int32, (blk, width), 0)
    rows = jnp.zeros((blk, width), f32)
    for i, part in enumerate(parts):
        rows = jnp.where(ids == i, part, rows)
    base_ref[start + blk : start + 2 * blk, :] = rows.astype(bf16)
    stores[3].start()
    for copy in stores:
        copy.wait()


def acceptor_kernel(blocks, blk, grad_ref, w_ref, slope_ref, out_ref):
    here = lax.axis_index("ctx")
    w = w_ref[...]
    width = w.shape[0]
    total = [None] * blocks
    for tile, (_, a) in enumerate(tiles_of(blocks)):
        grad_pair = lax.dot_general(
            grad_ref[tile], w, (((1,), (1,)), ((), ())), preferred_element_type=jnp.float32
        )
        part = jnp.sum((grad_pair * slope_ref[tile]).reshape(blk, blk, width), axis=0)
        total[a] = part if total[a] is None else total[a] + part
    for a in range(blocks):
        out_ref[a ^ here] = total[a]


def shared(
    donor_feat,
    acceptor_feat,
    donor_pos,
    acceptor_pos,
    pair_mask,
    targets,
    dist_table,
    hidden_weights,
    output_weights,
):
    _, blk, width = donor_feat.shape
    blocks = lax.axis_size("ctx")
    tissues, _, hidden = hidden_weights.shape
    bf16 = jnp.bfloat16
    f32 = jnp.float32
    anywhere = pl.BlockSpec(memory_space=pl.ANY)
    packed, base = pl.pallas_call(
        functools.partial(pack_kernel, blocks),
        in_specs=[anywhere] * 8,
        out_specs=[anywhere] * 2,
        out_shape=(
            jax.ShapeDtypeStruct((blk, 2 * width + LANES), bf16),
            jax.ShapeDtypeStruct((BINS + 4 * blk, width), bf16),
        ),
        scratch_shapes=[
            pltpu.SMEM(donor_pos.shape, jnp.int32),
            pltpu.SMEM((1, tissues, blk), jnp.int32),
            pltpu.SMEM(acceptor_pos.shape, jnp.int32),
            pltpu.VMEM(pair_mask.shape, jnp.int32),
            pltpu.VMEM((tissues, hidden), bf16),
            pltpu.VMEM((blk, LANES), bf16),
            pltpu.VMEM((BINS + 4 * blk, width), bf16),
            pltpu.SemaphoreType.DMA((12,)),
        ],
        compiler_params=pltpu.CompilerParams(vmem_limit_bytes=60 * 2**20),
        name="pack",
    )(
        donor_pos,
        jnp.transpose(targets, (0, 2, 1)),
        acceptor_pos,
        pair_mask,
        donor_feat,
        acceptor_feat,
        output_weights,
        dist_table,
    )
    base = halved(base)
    w_in = halved(lax.dynamic_index_in_dim(hidden_weights, lax.axis_index("ctx"), 0, False))
    pieces = [swapped(packed, "ctx", k) for k in GATHER_ORDER]
    tiles = len(tiles_of(blocks))
    chunk = width // (4 * blocks)
    pairs = blk * blk
    partial, loss, grad, slope = pl.pallas_call(
        functools.partial(head_kernel, blocks, blk, width),
        out_shape=(
            jax.ShapeDtypeStruct((2, 2, blocks, chunk, hidden), f32),
            jax.ShapeDtypeStruct((blocks, blk, LANES), f32),
            jax.ShapeDtypeStruct((tiles, pairs, hidden), bf16),
            jax.ShapeDtypeStruct((tiles, pairs, width), f32),
        ),
        scratch_shapes=[
            pltpu.VMEM((BINS + 2 * blocks * blk, width), bf16),
            pltpu.VMEM((blocks * blk, LANES), bf16),
            pltpu.VMEM((tiles, pairs, BINS), bf16),
            pltpu.VMEM((tiles, pairs, width), bf16),
            pltpu.VMEM((tiles, pairs, hidden), bf16),
            pltpu.VMEM((tiles, pairs, hidden), f32),
            pltpu.VMEM((width, hidden), f32),
        ],
        compiler_params=pltpu.CompilerParams(vmem_limit_bytes=32 * 2**20),
        name="head",
    )(base, w_in, *pieces)
    kept, sent = partial[0], swapped(partial[1], "rep", 1)
    acc = pl.pallas_call(
        functools.partial(acceptor_kernel, blocks, blk),
        out_shape=jax.ShapeDtypeStruct((blocks, blk, width), f32),
        compiler_params=pltpu.CompilerParams(vmem_limit_bytes=16 * 2**20),
        cost_estimate=pl.CostEstimate(
            flops=2 * tiles * pairs * width * hidden,
            bytes_accessed=tiles * pairs * (2 * hidden + 4 * width),
            transcendentals=0,
        ),
        name="acceptors",
    )(grad, w_in, slope)
    partial = kept + sent
    sent = swapped(partial[1].astype(bf16), "rep", 2)
    acc = acc + swapped(acc, "tis", 1)
    partial = partial[0] + sent.astype(jnp.float32)
    send = jnp.concatenate([partial, acc, loss], axis=2)
    arrived = [send[0]] + [swapped(send[k], "ctx", k) for k in RETURN_ORDER]
    donor_loss, grad_hidden, grad_acceptor = pl.pallas_call(
        functools.partial(finish_kernel, blocks, width, hidden),
        out_shape=(
            jax.ShapeDtypeStruct((1, tissues, blk), jnp.float32),
            jax.ShapeDtypeStruct((tissues, chunk, hidden), jnp.float32),
            jax.ShapeDtypeStruct((1, blk, width), jnp.float32),
        ),
        compiler_params=pltpu.CompilerParams(vmem_limit_bytes=8 * 2**20),
        name="finish",
    )(*arrived)
    return (jnp.transpose(donor_loss, (0, 2, 1)), grad_hidden, grad_acceptor)


def on_device(*args):
    donor_feat, acceptor_feat, _, _, pair_mask, _, _, hidden_weights, _ = args
    blocks = lax.axis_size("ctx")
    tissues, width, hidden = hidden_weights.shape
    blk = donor_feat.shape[1]
    fits = (
        donor_feat.shape[0] == 1
        and tissues == blocks == 4
        and lax.axis_size("rep") == 4
        and lax.axis_size("tis") == 2
        and acceptor_feat.shape[1] == blk == 16
        and width == 256
        and hidden % width == 0
        and pair_mask.shape[2] == (SPAN_BLOCKS + 1) * blk
        and BINS == LANES == 2 * blocks * blk
    )
    return shared(*args) if fits else general(*args)


def solution(mesh):
    placed = (
        P("rep", "ctx", None),
        P("rep", "ctx", None),
        P("rep", "ctx"),
        P("rep", None),
        P("rep", "ctx", None),
        P("rep", "ctx", "tis"),
        P(),
        P("tis", None, None),
        P("tis", None),
    )
    return jax.shard_map(
        on_device,
        mesh=mesh,
        in_specs=placed,
        out_specs=(P("rep", "ctx", "tis"), P("tis", ("ctx", "rep"), None), P("rep", "ctx", None)),
        check_vma=False,
    )
```

```python
import functools

import jax
import jax.numpy as jnp
from jax import lax
from jax.experimental import pallas as pl
from jax.experimental.pallas import tpu as pltpu
from jax.sharding import PartitionSpec as P

BLOCK_BP = 65536
SPAN_BLOCKS = 4
BIN_BP = 2048
BINS = 128
LANES = 128
GATHER_ORDER = (1, 3, 2)
RETURN_ORDER = (1, 3, 2)
LAGS = (10, 12, 13)


def passed_along(value, axis, steps):
    count = lax.axis_size(axis)
    first, last = (max(0, -steps), min(count, count - steps))
    return lax.ppermute(value, axis, [(source, source + steps) for source in range(first, last)])


def swapped(value, axis, bits):
    return lax.ppermute(value, axis, [(i, i ^ bits) for i in range(lax.axis_size(axis))])


def silu_grad(values):
    sig = jax.nn.sigmoid(values)
    return sig * (1.0 + values * (1.0 - sig))


def general(
    donor_feat,
    acceptor_feat,
    donor_pos,
    acceptor_pos,
    pair_mask,
    targets,
    dist_table,
    hidden_weights,
    output_weights,
):
    seq_dev, don_blk, width = donor_feat.shape
    acc_blk = acceptor_feat.shape[1]
    blocks = lax.axis_size("ctx")
    reach = SPAN_BLOCKS + 1
    slots = reach * acc_blk
    here = lax.axis_index("ctx")
    pieces = [acceptor_feat]
    for offset in range(1, reach):
        pieces.append(
            passed_along(acceptor_feat, "ctx", -offset)
            if offset < blocks
            else jnp.zeros_like(acceptor_feat)
        )
    window = jnp.stack(pieces, axis=1).reshape(seq_dev, slots, width)
    pos_pad = jnp.concatenate(
        [acceptor_pos, jnp.zeros((seq_dev, SPAN_BLOCKS * acc_blk), jnp.int32)], axis=1
    )
    pos_win = lax.dynamic_slice_in_dim(pos_pad, here * acc_blk, slots, 1)
    slot_block = jnp.arange(slots, dtype=jnp.int32) // acc_blk
    inchain = here + slot_block < blocks
    dist = slot_block * BLOCK_BP + pos_win[:, None, :] - donor_pos[:, :, None]
    valid = (pair_mask > 0) & (dist > 0) & (dist <= SPAN_BLOCKS * BLOCK_BP) & inchain[None, None, :]
    bins = jnp.clip((dist - 1) // BIN_BP, 0, BINS - 1)
    lookup = (
        (bins[..., None] == jnp.arange(BINS, dtype=jnp.int32))
        .astype(jnp.bfloat16)
        .reshape(-1, BINS)
    )
    table = jnp.dot(lookup, dist_table, preferred_element_type=jnp.float32).reshape(
        seq_dev, don_blk, slots, width
    )
    pre = (
        donor_feat.astype(jnp.float32)[:, :, None, :] + window.astype(jnp.float32)[:, None] + table
    )
    flat = jax.nn.silu(pre).astype(jnp.bfloat16).reshape(-1, width)
    grad_pair = jnp.zeros((flat.shape[0], width), jnp.float32)
    losses = []
    fulls = []
    slot_ids = jnp.arange(slots, dtype=jnp.int32)
    for tissue in range(hidden_weights.shape[0]):
        w_in = hidden_weights[tissue]
        w_out = output_weights[tissue]
        goal = targets[:, :, tissue]
        hid = jnp.dot(flat, w_in, preferred_element_type=jnp.float32)
        act = jax.nn.silu(hid).astype(jnp.bfloat16)
        logits = jnp.dot(act, w_out, preferred_element_type=jnp.float32).reshape(
            seq_dev, don_blk, slots
        )
        masked = jnp.where(valid, logits, -jnp.inf)
        top = jnp.maximum(jnp.max(masked, axis=-1), 0.0)
        expo = jnp.exp(masked - top[..., None])
        total = jnp.sum(expo, axis=-1) + jnp.exp(-top)
        onehot = goal[..., None] == slot_ids
        picked = jnp.sum(jnp.where(onehot, logits, 0.0), axis=-1)
        losses.append(top + jnp.log(total) - picked)
        grad_logits = expo / total[..., None] - onehot.astype(jnp.float32)
        grad_act = grad_logits.reshape(-1)[:, None] * w_out.astype(jnp.float32)[None, :]
        grad_hid = (grad_act * silu_grad(hid)).astype(jnp.bfloat16)
        grad_pair = grad_pair + lax.dot_general(
            grad_hid, w_in, (((1,), (1,)), ((), ())), preferred_element_type=jnp.float32
        )
        fulls.append(
            lax.dot_general(
                flat, grad_hid, (((0,), (0,)), ((), ())), preferred_element_type=jnp.float32
            )
        )
    stacked = jnp.stack(fulls, axis=1)
    grad_hidden = jnp.transpose(
        lax.psum_scatter(stacked, ("ctx", "rep"), scatter_dimension=0, tiled=True), (1, 0, 2)
    )
    grad_pre = grad_pair.reshape(seq_dev, don_blk, slots, width) * silu_grad(pre)
    contrib = jnp.sum(grad_pre, axis=1).reshape(seq_dev, reach, acc_blk, width)
    carried = contrib[:, 0]
    for offset in range(1, min(reach, blocks)):
        carried = carried + passed_along(contrib[:, offset], "ctx", offset)
    grad_acceptor = lax.psum(carried, "tis")
    donor_loss = jnp.stack(losses, axis=-1)
    return (donor_loss, grad_hidden, grad_acceptor)


def halved(value):
    return (value.astype(jnp.float32) * 0.5).astype(value.dtype)


def silu_parts(half):
    turn = jnp.tanh(half)
    tilted = half * turn
    return half + tilted, (1.0 + turn) * ((1.0 + half) - tilted)


def ones_dot(left, right):
    return jnp.dot(left, right, preferred_element_type=jnp.float32)


def tiles_of(blocks):
    return [(b, a) for b in range(blocks) for a in range(b, min(blocks, b + SPAN_BLOCKS + 1))]


def head_kernel(blocks, blk, width, *refs):
    (base_ref, w_ref) = refs[:2]
    packed = refs[2 : blocks + 2]
    (gh_ref, loss_ref, grad_s, dpre_s) = refs[blocks + 2 : blocks + 6]
    (source, aux, picks_s, pair_s, act_s, dhid_s, gh_s) = refs[blocks + 6 :]
    here = lax.axis_index("ctx")
    rep = lax.axis_index("rep")
    cross = lax.div(rep, 2)
    core = lax.rem(rep, 2)
    f32, bf16 = jnp.float32, jnp.bfloat16
    hidden = gh_s.shape[1]
    pairs = blk * blk
    sites = blocks * blk
    slots = (SPAN_BLOCKS + 1) * blk
    tiles = tiles_of(blocks)

    source[:BINS, :] = base_ref[:BINS, :]
    for piece, k in zip(packed, (0,) + GATHER_ORDER):
        start = pl.multiple_of((here ^ k) * blk, blk)
        source[pl.ds(BINS + start, blk), :] = halved(piece[:blk, :])
        source[pl.ds(BINS + sites + start, blk), :] = halved(piece[blk : 2 * blk, :])
        aux[pl.ds(start, blk), :] = piece[2 * blk :, :]

    lanes = lax.broadcasted_iota(jnp.int32, (blk, LANES), 1)
    ids = lax.broadcasted_iota(jnp.int32, (blk, LANES), 0)
    codes = []
    aims = []
    for b in range(blocks):
        extra = aux[b * blk : (b + 1) * blk, :].astype(f32)
        rows = extra[:, LANES:]

        def column(row):
            return jnp.sum(jnp.where(lanes == ids, row, 0.0), axis=1, keepdims=True)

        dpos = column(rows[:1, :] * 256.0 + rows[1:2, :])
        apos = rows[2:3, :] * 256.0 + rows[3:4, :]
        aim = column(
            jnp.sum(jnp.where(ids == here + 4, rows, 0.0), axis=0, keepdims=True)
        ).astype(jnp.int32)
        mask = pltpu.roll(extra[:, :LANES], b * blk, 1) if b else extra[:, :LANES]
        dist = (lanes // blk - b) * BLOCK_BP + (apos - dpos).astype(jnp.int32)
        valid = (mask > 0.5) & (dist > 0) & (dist <= SPAN_BLOCKS * BLOCK_BP) & (lanes < sites)
        code = jnp.where(valid, jnp.clip((dist - 1) // BIN_BP, 0, BINS - 1), -1)
        codes.append(code.astype(f32))
        aims.append(jnp.where(aim == slots, -1, aim + b * blk))

    w_half = w_ref[...]
    w_out = base_ref[BINS:, :].astype(f32)
    tissues = blocks
    ids = lax.broadcasted_iota(jnp.int32, w_out.shape, 0)
    w_out = jnp.concatenate(
        [
            jnp.sum(jnp.where(ids == here + part * tissues, w_out, 0.0), axis=0, keepdims=True)
            for part in range(hidden // width)
        ],
        axis=1,
    )
    w_rows = jnp.broadcast_to(w_out * 2.0, (LANES, hidden)).astype(bf16)
    ones = jnp.ones((LANES, LANES), bf16)
    lane3 = lax.broadcasted_iota(jnp.int32, (blk, blk, LANES), 2)
    row3 = lax.broadcasted_iota(jnp.int32, (blk, blk, LANES), 1)
    don3 = lax.broadcasted_iota(jnp.int32, (blk, blk, LANES), 0)
    lane_f = lax.broadcasted_iota(jnp.int32, (pairs, LANES), 1).astype(f32)
    from_donor = [
        jnp.where(lane3 == don3 + b * blk, 1.0, 0.0).astype(bf16).reshape(pairs, LANES)
        for b in range(blocks)
    ]
    from_acceptor = [
        jnp.where(lane3 == row3 + (sites + a * blk), 1.0, 0.0).astype(bf16).reshape(pairs, LANES)
        for a in range(blocks)
    ]
    slot_of = [lane3 == row3 + a * blk for a in range(blocks)]
    twice_of = [pick | (lane3 == row3 + (sites + a * blk)) for a, pick in enumerate(slot_of)]
    spread_out = [jnp.zeros((blk, blk, LANES), f32)] * blocks

    def bins_of(tile):
        b, a = tiles[tile]
        code = jnp.where(slot_of[a], codes[b][:, None, :], 0.0).astype(bf16)
        code = ones_dot(code.reshape(pairs, LANES), ones)
        picks_s[tile] = jnp.where(code == lane_f, 1.0, 0.0).astype(bf16)

    def pair_of(tile):
        b, a = tiles[tile]
        picks = jnp.concatenate([picks_s[tile], from_donor[b] + from_acceptor[a]], axis=1)
        value, slope = silu_parts(ones_dot(picks, source[...]))
        pair_s[tile] = value.astype(bf16)
        dpre_s[tile] = slope

    def hidden_of(tile):
        value, slope = silu_parts(ones_dot(pair_s[tile], w_half))
        act_s[tile] = value.astype(bf16)
        dhid_s[tile] = slope * w_out

    def logits_of(tile):
        b, a = tiles[tile]
        logit = lax.dot_general(
            act_s[tile], w_rows, (((1,), (1,)), ((), ())), preferred_element_type=f32
        )
        spread_out[b] = jnp.where(slot_of[a], logit.reshape(blk, blk, LANES), spread_out[b])

    stages = [(bins_of, 0), (pair_of, LAGS[0]), (hidden_of, LAGS[1]), (logits_of, LAGS[2])]
    for step in range(len(tiles) + stages[-1][1]):
        for stage, lag in stages:
            if 0 <= step - lag < len(tiles):
                stage(step - lag)
    grads = []
    for b in range(blocks):
        logit = jnp.sum(spread_out[b], axis=1)
        chosen = lanes == aims[b]
        masked = jnp.where(codes[b] >= 0.0, logit, -jnp.inf)
        top = jnp.maximum(jnp.max(masked, axis=1, keepdims=True), 0.0)
        expo = jnp.exp(masked - top)
        total = jnp.sum(expo, axis=1, keepdims=True) + jnp.exp(-top)
        picked = jnp.sum(jnp.where(chosen, logit, 0.0), axis=1, keepdims=True)
        loss_ref[b ^ here] = jnp.broadcast_to(top + jnp.log(total) - picked, (blk, LANES))
        grad = expo / total - jnp.where(chosen, 1.0, 0.0)
        high = grad.astype(bf16).astype(f32)
        grads.append(high + pltpu.roll(grad - high, sites, 1))
    def gradient_of(start, stop):
        count = (stop - start) * pairs
        return lax.dot_general(
            pair_s[start:stop].reshape(count, width),
            grad_s[start:stop].reshape(count, hidden),
            (((0,), (0,)), ((), ())),
            preferred_element_type=f32,
        )

    middle = len(tiles) // 2
    for tile, (b, a) in enumerate(tiles):
        rows = jnp.where(twice_of[a], grads[b][:, None, :], 0.0).astype(bf16)
        rows = ones_dot(rows.reshape(pairs, LANES), ones)
        rows = jnp.concatenate([rows] * (hidden // LANES), axis=1)
        grad_s[tile] = (rows * dhid_s[tile]).astype(bf16)
        if tile == middle:
            gh_s[...] = gradient_of(0, middle)
    total = gh_s[...] + gradient_of(middle, len(tiles))
    chunk = gh_ref.shape[3]
    for c in range(blocks):
        for x in range(2):
            for y in range(2):
                start = ((c * 2 + x) * 2 + y) * chunk
                gh_ref[y ^ core, x ^ cross, c ^ here] = total[start : start + chunk, :]


def finish_kernel(parts, width, hidden, *refs):
    pieces = refs[:parts]
    (loss_ref, gh_ref, acc_ref) = refs[parts:]
    here = lax.axis_index("ctx")
    blk = pieces[0].shape[0]
    total = None
    diagonal = lax.broadcasted_iota(jnp.int32, (blk, LANES), 0) == lax.broadcasted_iota(
        jnp.int32, (blk, LANES), 1
    )
    for piece, k in zip(pieces, (0,) + RETURN_ORDER):
        owner = here ^ k
        gh_ref[owner] = piece[:, :hidden]
        acc = piece[:, hidden : hidden + width]
        total = acc if total is None else total + acc
        row = jnp.sum(
            jnp.where(diagonal, piece[:, hidden + width :], 0.0), axis=0, keepdims=True
        )
        loss_ref[0, pl.ds(owner, 1), :] = row[:, :blk]
    acc_ref[0] = total


def acceptor_kernel(blocks, blk, grad_ref, w_ref, slope_ref, out_ref):
    here = lax.axis_index("ctx")
    w = w_ref[...]
    width = w.shape[0]
    total = [None] * blocks
    for tile, (_, a) in enumerate(tiles_of(blocks)):
        grad_pair = lax.dot_general(
            grad_ref[tile], w, (((1,), (1,)), ((), ())), preferred_element_type=jnp.float32
        )
        part = jnp.sum((grad_pair * slope_ref[tile]).reshape(blk, blk, width), axis=0)
        total[a] = part if total[a] is None else total[a] + part
    for a in range(blocks):
        out_ref[a ^ here] = total[a]


def shared(
    donor_feat,
    acceptor_feat,
    donor_pos,
    acceptor_pos,
    pair_mask,
    targets,
    dist_table,
    hidden_weights,
    output_weights,
):
    _, blk, width = donor_feat.shape
    blocks = lax.axis_size("ctx")
    tissues, _, hidden = hidden_weights.shape
    bf16 = jnp.bfloat16
    f32 = jnp.float32
    def placed(value, rows, row, lane=0):
        height, extent = value.shape
        room = ((row, rows - row - height, 0), (lane, width - lane - extent, 0))
        return lax.pad(value, jnp.zeros((), value.dtype), room)

    rows = 3 * blk
    last = 2 * blk
    whole = sum(
        placed(value, rows, row, lane)
        for value, row, lane in (
            (pair_mask[0], last, 0),
            (donor_pos, last, LANES),
            (donor_pos, last + 1, LANES),
            (acceptor_pos, last + 2, LANES),
            (acceptor_pos, last + 3, LANES),
            (jnp.transpose(targets, (0, 2, 1))[0], last + 4, LANES),
        )
    )
    row = lax.broadcasted_iota(jnp.int32, whole.shape, 0)
    lane = lax.broadcasted_iota(jnp.int32, whole.shape, 1)
    high = (lane >= LANES) & ((row == last) | (row == last + 2))
    whole = jnp.where(high, whole >> 8, whole & 255).astype(f32)
    sites = placed(donor_feat[0], rows, 0) + placed(acceptor_feat[0], rows, blk)
    packed = (sites.astype(f32) + whole).astype(bf16)
    base = 0.5 * sum(
        placed(value, BINS + blk, row, lane)
        for value, row, lane in (
            (dist_table, 0, 0),
            (output_weights, BINS, 0),
            (output_weights, BINS + tissues, -width),
        )
    )
    w_in = halved(lax.dynamic_index_in_dim(hidden_weights, lax.axis_index("ctx"), 0, False))
    pieces = [swapped(packed, "ctx", k) for k in GATHER_ORDER]
    tiles = len(tiles_of(blocks))
    chunk = width // (4 * blocks)
    pairs = blk * blk
    partial, loss, grad, slope = pl.pallas_call(
        functools.partial(head_kernel, blocks, blk, width),
        out_shape=(
            jax.ShapeDtypeStruct((2, 2, blocks, chunk, hidden), f32),
            jax.ShapeDtypeStruct((blocks, blk, LANES), f32),
            jax.ShapeDtypeStruct((tiles, pairs, hidden), bf16),
            jax.ShapeDtypeStruct((tiles, pairs, width), f32),
        ),
        scratch_shapes=[
            pltpu.VMEM((BINS + 2 * blocks * blk, width), bf16),
            pltpu.VMEM((blocks * blk, width), bf16),
            pltpu.VMEM((tiles, pairs, BINS), bf16),
            pltpu.VMEM((tiles, pairs, width), bf16),
            pltpu.VMEM((tiles, pairs, hidden), bf16),
            pltpu.VMEM((tiles, pairs, hidden), f32),
            pltpu.VMEM((width, hidden), f32),
        ],
        compiler_params=pltpu.CompilerParams(vmem_limit_bytes=32 * 2**20),
        name="head",
    )(base, w_in, packed, *pieces)
    kept, sent = partial[0], swapped(partial[1], "rep", 1)
    acc = pl.pallas_call(
        functools.partial(acceptor_kernel, blocks, blk),
        out_shape=jax.ShapeDtypeStruct((blocks, blk, width), f32),
        compiler_params=pltpu.CompilerParams(vmem_limit_bytes=16 * 2**20),
        cost_estimate=pl.CostEstimate(
            flops=2 * tiles * pairs * width * hidden,
            bytes_accessed=tiles * pairs * (2 * hidden + 4 * width),
            transcendentals=0,
        ),
        name="acceptors",
    )(grad, w_in, slope)
    partial = kept + sent
    sent = swapped(partial[1].astype(bf16), "rep", 2)
    acc = acc + swapped(acc, "tis", 1)
    partial = partial[0] + sent.astype(jnp.float32)
    send = jnp.concatenate([partial, acc, loss], axis=2)
    arrived = [send[0]] + [swapped(send[k], "ctx", k) for k in RETURN_ORDER]
    donor_loss, grad_hidden, grad_acceptor = pl.pallas_call(
        functools.partial(finish_kernel, blocks, width, hidden),
        out_shape=(
            jax.ShapeDtypeStruct((1, tissues, blk), jnp.float32),
            jax.ShapeDtypeStruct((tissues, chunk, hidden), jnp.float32),
            jax.ShapeDtypeStruct((1, blk, width), jnp.float32),
        ),
        compiler_params=pltpu.CompilerParams(vmem_limit_bytes=8 * 2**20),
        name="finish",
    )(*arrived)
    return (jnp.transpose(donor_loss, (0, 2, 1)), grad_hidden, grad_acceptor)


def on_device(*args):
    donor_feat, acceptor_feat, _, _, pair_mask, _, _, hidden_weights, _ = args
    blocks = lax.axis_size("ctx")
    tissues, width, hidden = hidden_weights.shape
    blk = donor_feat.shape[1]
    fits = (
        donor_feat.shape[0] == 1
        and tissues == blocks == 4
        and lax.axis_size("rep") == 4
        and lax.axis_size("tis") == 2
        and acceptor_feat.shape[1] == blk == 16
        and width == 256
        and hidden == 2 * width
        and pair_mask.shape[2] == (SPAN_BLOCKS + 1) * blk
        and BINS == LANES == 2 * blocks * blk
    )
    return shared(*args) if fits else general(*args)


def solution(mesh):
    placed = (
        P("rep", "ctx", None),
        P("rep", "ctx", None),
        P("rep", "ctx"),
        P("rep", None),
        P("rep", "ctx", None),
        P("rep", "ctx", "tis"),
        P(),
        P("tis", None, None),
        P("tis", None),
    )
    return jax.shard_map(
        on_device,
        mesh=mesh,
        in_specs=placed,
        out_specs=(P("rep", "ctx", "tis"), P("tis", ("ctx", "rep"), None), P("rep", "ctx", None)),
        check_vma=False,
    )
```

```python
import functools

import jax
import jax.numpy as jnp
from jax import lax
from jax.experimental import pallas as pl
from jax.experimental.pallas import tpu as pltpu
from jax.sharding import PartitionSpec as P

BLOCK_BP = 65536
SPAN_BLOCKS = 4
BIN_BP = 2048
BINS = 128
LANES = 128
GATHER_ORDER = (1, 3, 2)
RETURN_ORDER = (1, 3, 2)
LAGS = (10, 12, 13)


def passed_along(value, axis, steps):
    count = lax.axis_size(axis)
    first, last = (max(0, -steps), min(count, count - steps))
    return lax.ppermute(value, axis, [(source, source + steps) for source in range(first, last)])


def swapped(value, axis, bits):
    return lax.ppermute(value, axis, [(i, i ^ bits) for i in range(lax.axis_size(axis))])


def silu_grad(values):
    sig = jax.nn.sigmoid(values)
    return sig * (1.0 + values * (1.0 - sig))


def general(
    donor_feat,
    acceptor_feat,
    donor_pos,
    acceptor_pos,
    pair_mask,
    targets,
    dist_table,
    hidden_weights,
    output_weights,
):
    seq_dev, don_blk, width = donor_feat.shape
    acc_blk = acceptor_feat.shape[1]
    blocks = lax.axis_size("ctx")
    reach = SPAN_BLOCKS + 1
    slots = reach * acc_blk
    here = lax.axis_index("ctx")
    pieces = [acceptor_feat]
    for offset in range(1, reach):
        pieces.append(
            passed_along(acceptor_feat, "ctx", -offset)
            if offset < blocks
            else jnp.zeros_like(acceptor_feat)
        )
    window = jnp.stack(pieces, axis=1).reshape(seq_dev, slots, width)
    pos_pad = jnp.concatenate(
        [acceptor_pos, jnp.zeros((seq_dev, SPAN_BLOCKS * acc_blk), jnp.int32)], axis=1
    )
    pos_win = lax.dynamic_slice_in_dim(pos_pad, here * acc_blk, slots, 1)
    slot_block = jnp.arange(slots, dtype=jnp.int32) // acc_blk
    inchain = here + slot_block < blocks
    dist = slot_block * BLOCK_BP + pos_win[:, None, :] - donor_pos[:, :, None]
    valid = (pair_mask > 0) & (dist > 0) & (dist <= SPAN_BLOCKS * BLOCK_BP) & inchain[None, None, :]
    bins = jnp.clip((dist - 1) // BIN_BP, 0, BINS - 1)
    lookup = (
        (bins[..., None] == jnp.arange(BINS, dtype=jnp.int32))
        .astype(jnp.bfloat16)
        .reshape(-1, BINS)
    )
    table = jnp.dot(lookup, dist_table, preferred_element_type=jnp.float32).reshape(
        seq_dev, don_blk, slots, width
    )
    pre = (
        donor_feat.astype(jnp.float32)[:, :, None, :] + window.astype(jnp.float32)[:, None] + table
    )
    flat = jax.nn.silu(pre).astype(jnp.bfloat16).reshape(-1, width)
    grad_pair = jnp.zeros((flat.shape[0], width), jnp.float32)
    losses = []
    fulls = []
    slot_ids = jnp.arange(slots, dtype=jnp.int32)
    for tissue in range(hidden_weights.shape[0]):
        w_in = hidden_weights[tissue]
        w_out = output_weights[tissue]
        goal = targets[:, :, tissue]
        hid = jnp.dot(flat, w_in, preferred_element_type=jnp.float32)
        act = jax.nn.silu(hid).astype(jnp.bfloat16)
        logits = jnp.dot(act, w_out, preferred_element_type=jnp.float32).reshape(
            seq_dev, don_blk, slots
        )
        masked = jnp.where(valid, logits, -jnp.inf)
        top = jnp.maximum(jnp.max(masked, axis=-1), 0.0)
        expo = jnp.exp(masked - top[..., None])
        total = jnp.sum(expo, axis=-1) + jnp.exp(-top)
        onehot = goal[..., None] == slot_ids
        picked = jnp.sum(jnp.where(onehot, logits, 0.0), axis=-1)
        losses.append(top + jnp.log(total) - picked)
        grad_logits = expo / total[..., None] - onehot.astype(jnp.float32)
        grad_act = grad_logits.reshape(-1)[:, None] * w_out.astype(jnp.float32)[None, :]
        grad_hid = (grad_act * silu_grad(hid)).astype(jnp.bfloat16)
        grad_pair = grad_pair + lax.dot_general(
            grad_hid, w_in, (((1,), (1,)), ((), ())), preferred_element_type=jnp.float32
        )
        fulls.append(
            lax.dot_general(
                flat, grad_hid, (((0,), (0,)), ((), ())), preferred_element_type=jnp.float32
            )
        )
    stacked = jnp.stack(fulls, axis=1)
    grad_hidden = jnp.transpose(
        lax.psum_scatter(stacked, ("ctx", "rep"), scatter_dimension=0, tiled=True), (1, 0, 2)
    )
    grad_pre = grad_pair.reshape(seq_dev, don_blk, slots, width) * silu_grad(pre)
    contrib = jnp.sum(grad_pre, axis=1).reshape(seq_dev, reach, acc_blk, width)
    carried = contrib[:, 0]
    for offset in range(1, min(reach, blocks)):
        carried = carried + passed_along(contrib[:, offset], "ctx", offset)
    grad_acceptor = lax.psum(carried, "tis")
    donor_loss = jnp.stack(losses, axis=-1)
    return (donor_loss, grad_hidden, grad_acceptor)


def halved(value):
    return (value.astype(jnp.float32) * 0.5).astype(value.dtype)


def silu_parts(half):
    turn = jnp.tanh(half)
    value = half + half * turn
    return value, 2.0 - (1.0 - value) * (1.0 - turn)


def ones_dot(left, right):
    return jnp.dot(left, right, preferred_element_type=jnp.float32)


def tiles_of(blocks):
    return [(b, a) for b in range(blocks) for a in range(b, min(blocks, b + SPAN_BLOCKS + 1))]


def head_kernel(blocks, blk, width, *refs):
    (base_ref, w_ref) = refs[:2]
    packed = refs[2 : blocks + 2]
    (gh_ref, loss_ref, grad_s, dpre_s) = refs[blocks + 2 : blocks + 6]
    (source, aux, picks_s, pair_s, act_s, dhid_s, gh_s) = refs[blocks + 6 :]
    here = lax.axis_index("ctx")
    rep = lax.axis_index("rep")
    cross = lax.div(rep, 2)
    core = lax.rem(rep, 2)
    f32, bf16 = jnp.float32, jnp.bfloat16
    hidden = gh_s.shape[1]
    pairs = blk * blk
    sites = blocks * blk
    slots = (SPAN_BLOCKS + 1) * blk
    tiles = tiles_of(blocks)

    source[:BINS, :] = base_ref[:BINS, :]
    for piece, k in zip(packed, (0,) + GATHER_ORDER):
        start = pl.multiple_of((here ^ k) * blk, blk)
        source[pl.ds(BINS + start, blk), :] = halved(piece[:blk, :])
        source[pl.ds(BINS + sites + start, blk), :] = halved(piece[blk : 2 * blk, :])
        aux[pl.ds(start, blk), :] = piece[2 * blk :, :]

    lanes = lax.broadcasted_iota(jnp.int32, (blk, LANES), 1)
    ids = lax.broadcasted_iota(jnp.int32, (blk, LANES), 0)
    codes = []
    aims = []
    for b in range(blocks):
        extra = aux[b * blk : (b + 1) * blk, :].astype(f32)
        rows = extra[:, LANES:]

        def column(row):
            return jnp.sum(jnp.where(lanes == ids, row, 0.0), axis=1, keepdims=True)

        dpos = column(rows[:1, :] * 256.0 + rows[1:2, :])
        apos = rows[2:3, :] * 256.0 + rows[3:4, :]
        aim = column(
            jnp.sum(jnp.where(ids == here + 4, rows, 0.0), axis=0, keepdims=True)
        ).astype(jnp.int32)
        mask = pltpu.roll(extra[:, :LANES], b * blk, 1) if b else extra[:, :LANES]
        dist = (lanes // blk - b) * BLOCK_BP + (apos - dpos).astype(jnp.int32)
        valid = (mask > 0.5) & (dist > 0) & (dist <= SPAN_BLOCKS * BLOCK_BP) & (lanes < sites)
        code = jnp.where(valid, jnp.clip((dist - 1) // BIN_BP, 0, BINS - 1), -1)
        codes.append(code.astype(f32))
        aims.append(jnp.where(aim == slots, -1, aim + b * blk))

    w_half = w_ref[...]
    w_out = base_ref[BINS:, :].astype(f32)
    tissues = blocks
    ids = lax.broadcasted_iota(jnp.int32, w_out.shape, 0)
    w_out = jnp.concatenate(
        [
            jnp.sum(jnp.where(ids == here + part * tissues, w_out, 0.0), axis=0, keepdims=True)
            for part in range(hidden // width)
        ],
        axis=1,
    )
    w_rows = jnp.broadcast_to(w_out * 2.0, (LANES, hidden)).astype(bf16)
    ones = jnp.ones((LANES, LANES), bf16)
    lane3 = lax.broadcasted_iota(jnp.int32, (blk, blk, LANES), 2)
    row3 = lax.broadcasted_iota(jnp.int32, (blk, blk, LANES), 1)
    don3 = lax.broadcasted_iota(jnp.int32, (blk, blk, LANES), 0)
    lane_f = lax.broadcasted_iota(jnp.int32, (pairs, LANES), 1).astype(f32)
    from_donor = [
        jnp.where(lane3 == don3 + b * blk, 1.0, 0.0).astype(bf16).reshape(pairs, LANES)
        for b in range(blocks)
    ]
    from_acceptor = [
        jnp.where(lane3 == row3 + (sites + a * blk), 1.0, 0.0).astype(bf16).reshape(pairs, LANES)
        for a in range(blocks)
    ]
    slot_of = [lane3 == row3 + a * blk for a in range(blocks)]
    twice_of = [pick | (lane3 == row3 + (sites + a * blk)) for a, pick in enumerate(slot_of)]
    spread_out = [jnp.zeros((blk, blk, LANES), f32)] * blocks

    def bins_of(tile):
        b, a = tiles[tile]
        code = jnp.where(slot_of[a], codes[b][:, None, :], 0.0).astype(bf16)
        code = ones_dot(code.reshape(pairs, LANES), ones)
        picks_s[tile] = jnp.where(code == lane_f, 1.0, 0.0).astype(bf16)

    def pair_of(tile):
        b, a = tiles[tile]
        picks = jnp.concatenate([picks_s[tile], from_donor[b] + from_acceptor[a]], axis=1)
        value, slope = silu_parts(ones_dot(picks, source[...]))
        pair_s[tile] = value.astype(bf16)
        dpre_s[tile] = slope

    def hidden_of(tile):
        value, slope = silu_parts(ones_dot(pair_s[tile], w_half))
        act_s[tile] = value.astype(bf16)
        dhid_s[tile] = slope * w_out

    def logits_of(tile):
        b, a = tiles[tile]
        logit = lax.dot_general(
            act_s[tile], w_rows, (((1,), (1,)), ((), ())), preferred_element_type=f32
        )
        spread_out[b] = jnp.where(slot_of[a], logit.reshape(blk, blk, LANES), spread_out[b])

    stages = [(bins_of, 0), (pair_of, LAGS[0]), (hidden_of, LAGS[1]), (logits_of, LAGS[2])]
    for step in range(len(tiles) + stages[-1][1]):
        for stage, lag in stages:
            if 0 <= step - lag < len(tiles):
                stage(step - lag)
    grads = []
    for b in range(blocks):
        logit = jnp.sum(spread_out[b], axis=1)
        chosen = lanes == aims[b]
        masked = jnp.where(codes[b] >= 0.0, logit, -jnp.inf)
        top = jnp.maximum(jnp.max(masked, axis=1, keepdims=True), 0.0)
        expo = jnp.exp(masked - top)
        total = jnp.sum(expo, axis=1, keepdims=True) + jnp.exp(-top)
        picked = jnp.sum(jnp.where(chosen, logit, 0.0), axis=1, keepdims=True)
        loss_ref[b ^ here] = jnp.broadcast_to(top + jnp.log(total) - picked, (blk, LANES))
        grad = expo / total - jnp.where(chosen, 1.0, 0.0)
        high = grad.astype(bf16).astype(f32)
        grads.append(high + pltpu.roll(grad - high, sites, 1))
    def gradient_of(start, stop):
        count = (stop - start) * pairs
        return lax.dot_general(
            pair_s[start:stop].reshape(count, width),
            grad_s[start:stop].reshape(count, hidden),
            (((0,), (0,)), ((), ())),
            preferred_element_type=f32,
        )

    middle = len(tiles) // 2
    for tile, (b, a) in enumerate(tiles):
        rows = jnp.where(twice_of[a], grads[b][:, None, :], 0.0).astype(bf16)
        rows = ones_dot(rows.reshape(pairs, LANES), ones)
        rows = jnp.concatenate([rows] * (hidden // LANES), axis=1)
        grad_s[tile] = (rows * dhid_s[tile]).astype(bf16)
        if tile == middle:
            gh_s[...] = gradient_of(0, middle)
    total = gh_s[...] + gradient_of(middle, len(tiles))
    chunk = gh_ref.shape[3]
    for c in range(blocks):
        for x in range(2):
            for y in range(2):
                start = ((c * 2 + x) * 2 + y) * chunk
                gh_ref[y ^ core, x ^ cross, c ^ here] = total[start : start + chunk, :]


def finish_kernel(parts, width, hidden, *refs):
    pieces = refs[:parts]
    (loss_ref, gh_ref, acc_ref) = refs[parts:]
    here = lax.axis_index("ctx")
    blk = pieces[0].shape[0]
    total = None
    diagonal = lax.broadcasted_iota(jnp.int32, (blk, LANES), 0) == lax.broadcasted_iota(
        jnp.int32, (blk, LANES), 1
    )
    for piece, k in zip(pieces, (0,) + RETURN_ORDER):
        owner = here ^ k
        gh_ref[owner] = piece[:, :hidden]
        acc = piece[:, hidden : hidden + width]
        total = acc if total is None else total + acc
        row = jnp.sum(
            jnp.where(diagonal, piece[:, hidden + width :], 0.0), axis=0, keepdims=True
        )
        loss_ref[0, pl.ds(owner, 1), :] = row[:, :blk]
    acc_ref[0] = total


def acceptor_kernel(blocks, blk, grad_ref, w_ref, slope_ref, out_ref):
    here = lax.axis_index("ctx")
    w = w_ref[...]
    width = w.shape[0]
    total = [None] * blocks
    for tile, (_, a) in enumerate(tiles_of(blocks)):
        grad_pair = lax.dot_general(
            grad_ref[tile], w, (((1,), (1,)), ((), ())), preferred_element_type=jnp.float32
        )
        part = jnp.sum((grad_pair * slope_ref[tile]).reshape(blk, blk, width), axis=0)
        total[a] = part if total[a] is None else total[a] + part
    for a in range(blocks):
        out_ref[a ^ here] = total[a]


def shared(
    donor_feat,
    acceptor_feat,
    donor_pos,
    acceptor_pos,
    pair_mask,
    targets,
    dist_table,
    hidden_weights,
    output_weights,
):
    _, blk, width = donor_feat.shape
    blocks = lax.axis_size("ctx")
    tissues, _, hidden = hidden_weights.shape
    bf16 = jnp.bfloat16
    f32 = jnp.float32
    def placed(value, rows, row, lane=0):
        height, extent = value.shape
        room = ((row, rows - row - height, 0), (lane, width - lane - extent, 0))
        return lax.pad(value, jnp.zeros((), value.dtype), room)

    rows = 3 * blk
    last = 2 * blk
    whole = sum(
        placed(value, rows, row, lane)
        for value, row, lane in (
            (pair_mask[0], last, 0),
            (donor_pos, last, LANES),
            (donor_pos, last + 1, LANES),
            (acceptor_pos, last + 2, LANES),
            (acceptor_pos, last + 3, LANES),
            (jnp.transpose(targets, (0, 2, 1))[0], last + 4, LANES),
        )
    )
    row = lax.broadcasted_iota(jnp.int32, whole.shape, 0)
    lane = lax.broadcasted_iota(jnp.int32, whole.shape, 1)
    high = (lane >= LANES) & ((row == last) | (row == last + 2))
    whole = jnp.where(high, whole >> 8, whole & 255).astype(f32)
    sites = placed(donor_feat[0], rows, 0) + placed(acceptor_feat[0], rows, blk)
    packed = (sites.astype(f32) + whole).astype(bf16)
    base = 0.5 * sum(
        placed(value, BINS + blk, row, lane)
        for value, row, lane in (
            (dist_table, 0, 0),
            (output_weights, BINS, 0),
            (output_weights, BINS + tissues, -width),
        )
    )
    w_in = halved(lax.dynamic_index_in_dim(hidden_weights, lax.axis_index("ctx"), 0, False))
    pieces = [swapped(packed, "ctx", k) for k in GATHER_ORDER]
    tiles = len(tiles_of(blocks))
    chunk = width // (4 * blocks)
    pairs = blk * blk
    partial, loss, grad, slope = pl.pallas_call(
        functools.partial(head_kernel, blocks, blk, width),
        out_shape=(
            jax.ShapeDtypeStruct((2, 2, blocks, chunk, hidden), f32),
            jax.ShapeDtypeStruct((blocks, blk, LANES), f32),
            jax.ShapeDtypeStruct((tiles, pairs, hidden), bf16),
            jax.ShapeDtypeStruct((tiles, pairs, width), f32),
        ),
        scratch_shapes=[
            pltpu.VMEM((BINS + 2 * blocks * blk, width), bf16),
            pltpu.VMEM((blocks * blk, width), bf16),
            pltpu.VMEM((tiles, pairs, BINS), bf16),
            pltpu.VMEM((tiles, pairs, width), bf16),
            pltpu.VMEM((tiles, pairs, hidden), bf16),
            pltpu.VMEM((tiles, pairs, hidden), f32),
            pltpu.VMEM((width, hidden), f32),
        ],
        compiler_params=pltpu.CompilerParams(vmem_limit_bytes=32 * 2**20),
        name="head",
    )(base, w_in, packed, *pieces)
    kept, sent = partial[0], swapped(partial[1], "rep", 1)
    acc = pl.pallas_call(
        functools.partial(acceptor_kernel, blocks, blk),
        out_shape=jax.ShapeDtypeStruct((blocks, blk, width), f32),
        compiler_params=pltpu.CompilerParams(vmem_limit_bytes=16 * 2**20),
        cost_estimate=pl.CostEstimate(
            flops=2 * tiles * pairs * width * hidden,
            bytes_accessed=tiles * pairs * (2 * hidden + 4 * width),
            transcendentals=0,
        ),
        name="acceptors",
    )(grad, w_in, slope)
    partial = kept + sent
    sent = swapped(partial[1].astype(bf16), "rep", 2)
    acc = acc + swapped(acc, "tis", 1)
    partial = partial[0] + sent.astype(jnp.float32)
    send = jnp.concatenate([partial, acc, loss], axis=2)
    arrived = [send[0]] + [swapped(send[k], "ctx", k) for k in RETURN_ORDER]
    donor_loss, grad_hidden, grad_acceptor = pl.pallas_call(
        functools.partial(finish_kernel, blocks, width, hidden),
        out_shape=(
            jax.ShapeDtypeStruct((1, tissues, blk), jnp.float32),
            jax.ShapeDtypeStruct((tissues, chunk, hidden), jnp.float32),
            jax.ShapeDtypeStruct((1, blk, width), jnp.float32),
        ),
        compiler_params=pltpu.CompilerParams(vmem_limit_bytes=8 * 2**20),
        name="finish",
    )(*arrived)
    return (jnp.transpose(donor_loss, (0, 2, 1)), grad_hidden, grad_acceptor)


def on_device(*args):
    donor_feat, acceptor_feat, _, _, pair_mask, _, _, hidden_weights, _ = args
    blocks = lax.axis_size("ctx")
    tissues, width, hidden = hidden_weights.shape
    blk = donor_feat.shape[1]
    fits = (
        donor_feat.shape[0] == 1
        and tissues == blocks == 4
        and lax.axis_size("rep") == 4
        and lax.axis_size("tis") == 2
        and acceptor_feat.shape[1] == blk == 16
        and width == 256
        and hidden == 2 * width
        and pair_mask.shape[2] == (SPAN_BLOCKS + 1) * blk
        and BINS == LANES == 2 * blocks * blk
    )
    return shared(*args) if fits else general(*args)


def solution(mesh):
    placed = (
        P("rep", "ctx", None),
        P("rep", "ctx", None),
        P("rep", "ctx"),
        P("rep", None),
        P("rep", "ctx", None),
        P("rep", "ctx", "tis"),
        P(),
        P("tis", None, None),
        P("tis", None),
    )
    return jax.shard_map(
        on_device,
        mesh=mesh,
        in_specs=placed,
        out_specs=(P("rep", "ctx", "tis"), P("tis", ("ctx", "rep"), None), P("rep", "ctx", None)),
        check_vma=False,
    )
```

```python
import functools

import jax
import jax.numpy as jnp
from jax import lax
from jax.experimental import pallas as pl
from jax.experimental.pallas import tpu as pltpu
from jax.sharding import PartitionSpec as P

BLOCK_BP = 65536
SPAN_BLOCKS = 4
BIN_BP = 2048
BINS = 128
LANES = 128
GATHER_ORDER = (1, 3, 2)
RETURN_ORDER = (1, 3, 2)
LAGS = (10, 12, 13)


def passed_along(value, axis, steps):
    count = lax.axis_size(axis)
    first, last = (max(0, -steps), min(count, count - steps))
    return lax.ppermute(value, axis, [(source, source + steps) for source in range(first, last)])


def swapped(value, axis, bits):
    return lax.ppermute(value, axis, [(i, i ^ bits) for i in range(lax.axis_size(axis))])


def silu_grad(values):
    sig = jax.nn.sigmoid(values)
    return sig * (1.0 + values * (1.0 - sig))


def general(
    donor_feat,
    acceptor_feat,
    donor_pos,
    acceptor_pos,
    pair_mask,
    targets,
    dist_table,
    hidden_weights,
    output_weights,
):
    seq_dev, don_blk, width = donor_feat.shape
    acc_blk = acceptor_feat.shape[1]
    blocks = lax.axis_size("ctx")
    reach = SPAN_BLOCKS + 1
    slots = reach * acc_blk
    here = lax.axis_index("ctx")
    pieces = [acceptor_feat]
    for offset in range(1, reach):
        pieces.append(
            passed_along(acceptor_feat, "ctx", -offset)
            if offset < blocks
            else jnp.zeros_like(acceptor_feat)
        )
    window = jnp.stack(pieces, axis=1).reshape(seq_dev, slots, width)
    pos_pad = jnp.concatenate(
        [acceptor_pos, jnp.zeros((seq_dev, SPAN_BLOCKS * acc_blk), jnp.int32)], axis=1
    )
    pos_win = lax.dynamic_slice_in_dim(pos_pad, here * acc_blk, slots, 1)
    slot_block = jnp.arange(slots, dtype=jnp.int32) // acc_blk
    inchain = here + slot_block < blocks
    dist = slot_block * BLOCK_BP + pos_win[:, None, :] - donor_pos[:, :, None]
    valid = (pair_mask > 0) & (dist > 0) & (dist <= SPAN_BLOCKS * BLOCK_BP) & inchain[None, None, :]
    bins = jnp.clip((dist - 1) // BIN_BP, 0, BINS - 1)
    lookup = (
        (bins[..., None] == jnp.arange(BINS, dtype=jnp.int32))
        .astype(jnp.bfloat16)
        .reshape(-1, BINS)
    )
    table = jnp.dot(lookup, dist_table, preferred_element_type=jnp.float32).reshape(
        seq_dev, don_blk, slots, width
    )
    pre = (
        donor_feat.astype(jnp.float32)[:, :, None, :] + window.astype(jnp.float32)[:, None] + table
    )
    flat = jax.nn.silu(pre).astype(jnp.bfloat16).reshape(-1, width)
    grad_pair = jnp.zeros((flat.shape[0], width), jnp.float32)
    losses = []
    fulls = []
    slot_ids = jnp.arange(slots, dtype=jnp.int32)
    for tissue in range(hidden_weights.shape[0]):
        w_in = hidden_weights[tissue]
        w_out = output_weights[tissue]
        goal = targets[:, :, tissue]
        hid = jnp.dot(flat, w_in, preferred_element_type=jnp.float32)
        act = jax.nn.silu(hid).astype(jnp.bfloat16)
        logits = jnp.dot(act, w_out, preferred_element_type=jnp.float32).reshape(
            seq_dev, don_blk, slots
        )
        masked = jnp.where(valid, logits, -jnp.inf)
        top = jnp.maximum(jnp.max(masked, axis=-1), 0.0)
        expo = jnp.exp(masked - top[..., None])
        total = jnp.sum(expo, axis=-1) + jnp.exp(-top)
        onehot = goal[..., None] == slot_ids
        picked = jnp.sum(jnp.where(onehot, logits, 0.0), axis=-1)
        losses.append(top + jnp.log(total) - picked)
        grad_logits = expo / total[..., None] - onehot.astype(jnp.float32)
        grad_act = grad_logits.reshape(-1)[:, None] * w_out.astype(jnp.float32)[None, :]
        grad_hid = (grad_act * silu_grad(hid)).astype(jnp.bfloat16)
        grad_pair = grad_pair + lax.dot_general(
            grad_hid, w_in, (((1,), (1,)), ((), ())), preferred_element_type=jnp.float32
        )
        fulls.append(
            lax.dot_general(
                flat, grad_hid, (((0,), (0,)), ((), ())), preferred_element_type=jnp.float32
            )
        )
    stacked = jnp.stack(fulls, axis=1)
    grad_hidden = jnp.transpose(
        lax.psum_scatter(stacked, ("ctx", "rep"), scatter_dimension=0, tiled=True), (1, 0, 2)
    )
    grad_pre = grad_pair.reshape(seq_dev, don_blk, slots, width) * silu_grad(pre)
    contrib = jnp.sum(grad_pre, axis=1).reshape(seq_dev, reach, acc_blk, width)
    carried = contrib[:, 0]
    for offset in range(1, min(reach, blocks)):
        carried = carried + passed_along(contrib[:, offset], "ctx", offset)
    grad_acceptor = lax.psum(carried, "tis")
    donor_loss = jnp.stack(losses, axis=-1)
    return (donor_loss, grad_hidden, grad_acceptor)


def halved(value):
    return (value.astype(jnp.float32) * 0.5).astype(value.dtype)


def silu_parts(half):
    turn = jnp.tanh(half)
    value = half + half * turn
    return value, 2.0 - (1.0 - value) * (1.0 - turn)


def ones_dot(left, right):
    return jnp.dot(left, right, preferred_element_type=jnp.float32)


def tiles_of(blocks):
    return [(b, a) for b in range(blocks) for a in range(b, min(blocks, b + SPAN_BLOCKS + 1))]


def head_kernel(blocks, blk, width, *refs):
    (base_ref, w_ref) = refs[:2]
    packed = refs[2 : blocks + 2]
    (gh_ref, loss_ref, grad_s, dpre_s) = refs[blocks + 2 : blocks + 6]
    (source, aux, picks_s, pair_s, act_s, dhid_s, gh_s) = refs[blocks + 6 :]
    here = lax.axis_index("ctx")
    rep = lax.axis_index("rep")
    cross = lax.div(rep, 2)
    core = lax.rem(rep, 2)
    f32, bf16 = jnp.float32, jnp.bfloat16
    hidden = gh_s.shape[1]
    pairs = blk * blk
    sites = blocks * blk
    slots = (SPAN_BLOCKS + 1) * blk
    tiles = tiles_of(blocks)

    source[:BINS, :] = base_ref[:BINS, :]
    for piece, k in zip(packed, (0,) + GATHER_ORDER):
        start = pl.multiple_of((here ^ k) * blk, blk)
        source[pl.ds(BINS + start, blk), :] = halved(piece[:blk, :])
        source[pl.ds(BINS + sites + start, blk), :] = halved(piece[blk : 2 * blk, :])
        aux[pl.ds(start, blk), :] = piece[2 * blk :, :]

    lanes = lax.broadcasted_iota(jnp.int32, (blk, LANES), 1)
    ids = lax.broadcasted_iota(jnp.int32, (blk, LANES), 0)
    spots = base_ref[BINS:, :LANES].astype(f32)
    apos = spots[2 * blocks : 2 * blocks + 1, :] * 256.0
    apos = apos + spots[2 * blocks + 1 : 2 * blocks + 2, :]
    codes = []
    aims = []
    for b in range(blocks):
        extra = aux[b * blk : (b + 1) * blk, :].astype(f32)
        rows = extra[:, LANES:]

        def column(row):
            return jnp.sum(jnp.where(lanes == ids, row, 0.0), axis=1, keepdims=True)

        dpos = column(rows[:1, :] * 256.0 + rows[1:2, :])
        aim = column(
            jnp.sum(jnp.where(ids == here + 4, rows, 0.0), axis=0, keepdims=True)
        ).astype(jnp.int32)
        mask = pltpu.roll(extra[:, :LANES], b * blk, 1) if b else extra[:, :LANES]
        dist = (lanes // blk - b) * BLOCK_BP + (apos - dpos).astype(jnp.int32)
        valid = (mask > 0.5) & (dist > 0) & (dist <= SPAN_BLOCKS * BLOCK_BP) & (lanes < sites)
        code = jnp.where(valid, jnp.clip((dist - 1) // BIN_BP, 0, BINS - 1), -1)
        codes.append(code.astype(f32))
        aims.append(jnp.where(aim == slots, -1, aim + b * blk))

    w_half = w_ref[...]
    w_out = base_ref[BINS:, :].astype(f32)
    tissues = blocks
    row_ids = lax.broadcasted_iota(jnp.int32, w_out.shape, 0)
    w_out = jnp.concatenate(
        [
            jnp.sum(jnp.where(row_ids == here + part * tissues, w_out, 0.0), axis=0, keepdims=True)
            for part in range(hidden // width)
        ],
        axis=1,
    )
    w_rows = jnp.broadcast_to(w_out * 2.0, (LANES, hidden)).astype(bf16)
    ones = jnp.ones((LANES, LANES), bf16)
    lane3 = lax.broadcasted_iota(jnp.int32, (blk, blk, LANES), 2)
    row3 = lax.broadcasted_iota(jnp.int32, (blk, blk, LANES), 1)
    don3 = lax.broadcasted_iota(jnp.int32, (blk, blk, LANES), 0)
    lane_f = lax.broadcasted_iota(jnp.int32, (pairs, LANES), 1).astype(f32)
    from_donor = [
        jnp.where(lane3 == don3 + b * blk, 1.0, 0.0).astype(bf16).reshape(pairs, LANES)
        for b in range(blocks)
    ]
    from_acceptor = [
        jnp.where(lane3 == row3 + (sites + a * blk), 1.0, 0.0).astype(bf16).reshape(pairs, LANES)
        for a in range(blocks)
    ]
    slot_of = [lane3 == row3 + a * blk for a in range(blocks)]
    twice_of = [pick | (lane3 == row3 + (sites + a * blk)) for a, pick in enumerate(slot_of)]
    spread_out = [jnp.zeros((blk, blk, LANES), f32)] * blocks

    def bins_of(tile):
        b, a = tiles[tile]
        code = jnp.where(slot_of[a], codes[b][:, None, :], 0.0).astype(bf16)
        code = ones_dot(code.reshape(pairs, LANES), ones)
        picks_s[tile] = jnp.where(code == lane_f, 1.0, 0.0).astype(bf16)

    def pair_of(tile):
        b, a = tiles[tile]
        picks = jnp.concatenate([picks_s[tile], from_donor[b] + from_acceptor[a]], axis=1)
        value, slope = silu_parts(ones_dot(picks, source[...]))
        pair_s[tile] = value.astype(bf16)
        dpre_s[tile] = slope

    def hidden_of(tile):
        value, slope = silu_parts(ones_dot(pair_s[tile], w_half))
        act_s[tile] = value.astype(bf16)
        dhid_s[tile] = slope * w_out

    def logits_of(tile):
        b, a = tiles[tile]
        logit = lax.dot_general(
            act_s[tile], w_rows, (((1,), (1,)), ((), ())), preferred_element_type=f32
        )
        spread_out[b] = jnp.where(slot_of[a], logit.reshape(blk, blk, LANES), spread_out[b])

    stages = [(bins_of, 0), (pair_of, LAGS[0]), (hidden_of, LAGS[1]), (logits_of, LAGS[2])]
    for step in range(len(tiles) + stages[-1][1]):
        for stage, lag in stages:
            if 0 <= step - lag < len(tiles):
                stage(step - lag)
    grads = []
    for b in range(blocks):
        logit = jnp.sum(spread_out[b], axis=1)
        chosen = lanes == aims[b]
        masked = jnp.where(codes[b] >= 0.0, logit, -jnp.inf)
        top = jnp.maximum(jnp.max(masked, axis=1, keepdims=True), 0.0)
        expo = jnp.exp(masked - top)
        total = jnp.sum(expo, axis=1, keepdims=True) + jnp.exp(-top)
        picked = jnp.sum(jnp.where(chosen, logit, 0.0), axis=1, keepdims=True)
        loss = jnp.where(lanes == ids, top + jnp.log(total) - picked, 0.0)
        loss = jnp.sum(loss, axis=0, keepdims=True)
        loss_ref[b ^ here] = jnp.broadcast_to(loss, loss_ref.shape[1:])
        grad = expo / total - jnp.where(chosen, 1.0, 0.0)
        high = grad.astype(bf16).astype(f32)
        grads.append(high + pltpu.roll(grad - high, sites, 1))
    def gradient_of(start, stop):
        count = (stop - start) * pairs
        return lax.dot_general(
            pair_s[start:stop].reshape(count, width),
            grad_s[start:stop].reshape(count, hidden),
            (((0,), (0,)), ((), ())),
            preferred_element_type=f32,
        )

    middle = len(tiles) // 2
    for tile, (b, a) in enumerate(tiles):
        rows = jnp.where(twice_of[a], grads[b][:, None, :], 0.0).astype(bf16)
        rows = ones_dot(rows.reshape(pairs, LANES), ones)
        rows = jnp.concatenate([rows] * (hidden // LANES), axis=1)
        grad_s[tile] = (rows * dhid_s[tile]).astype(bf16)
        if tile == middle:
            gh_s[...] = gradient_of(0, middle)
    total = gh_s[...] + gradient_of(middle, len(tiles))
    chunk = gh_ref.shape[3]
    for c in range(blocks):
        for x in range(2):
            for y in range(2):
                start = ((c * 2 + x) * 2 + y) * chunk
                gh_ref[y ^ core, x ^ cross, c ^ here] = total[start : start + chunk, :]


def finish_kernel(parts, width, hidden, *refs):
    pieces = refs[:parts]
    (loss_ref, gh_ref, acc_ref) = refs[parts:]
    here = lax.axis_index("ctx")
    blk = acc_ref.shape[1]
    total = None
    for piece, k in zip(pieces, (0,) + RETURN_ORDER):
        owner = here ^ k
        groups = (hidden + width) // LANES
        cuts = [piece[i * blk : (i + 1) * blk, :] for i in range(groups)]
        gh_ref[owner] = jnp.concatenate(cuts[: hidden // LANES], axis=1)
        acc = jnp.concatenate(cuts[hidden // LANES :], axis=1)
        total = acc if total is None else total + acc
        loss_ref[0, pl.ds(owner, 1), :] = piece[groups * blk : groups * blk + 1, :blk]
    acc_ref[0] = total


def acceptor_kernel(blocks, blk, grad_ref, w_ref, slope_ref, out_ref):
    here = lax.axis_index("ctx")
    w = w_ref[...]
    width = w.shape[0]
    total = [None] * blocks
    for tile, (_, a) in enumerate(tiles_of(blocks)):
        grad_pair = lax.dot_general(
            grad_ref[tile], w, (((1,), (1,)), ((), ())), preferred_element_type=jnp.float32
        )
        part = jnp.sum((grad_pair * slope_ref[tile]).reshape(blk, blk, width), axis=0)
        total[a] = part if total[a] is None else total[a] + part
    for a in range(blocks):
        out_ref[a ^ here] = total[a]


def shared(
    donor_feat,
    acceptor_feat,
    donor_pos,
    acceptor_pos,
    pair_mask,
    targets,
    dist_table,
    hidden_weights,
    output_weights,
):
    _, blk, width = donor_feat.shape
    blocks = lax.axis_size("ctx")
    tissues, _, hidden = hidden_weights.shape
    bf16 = jnp.bfloat16
    f32 = jnp.float32
    def placed(value, rows, row, lane=0):
        height, extent = value.shape
        room = ((row, rows - row - height, 0), (lane, width - lane - extent, 0))
        return lax.pad(value, jnp.zeros((), value.dtype), room)

    rows = 3 * blk
    last = 2 * blk
    whole = sum(
        placed(value, rows, row, lane)
        for value, row, lane in (
            (pair_mask[0], last, 0),
            (donor_pos, last, LANES),
            (donor_pos, last + 1, LANES),
            (jnp.transpose(targets, (0, 2, 1))[0], last + 4, LANES),
        )
    )
    row = lax.broadcasted_iota(jnp.int32, whole.shape, 0)
    lane = lax.broadcasted_iota(jnp.int32, whole.shape, 1)
    whole = jnp.where((lane >= LANES) & (row == last), whole >> 8, whole & 255).astype(f32)
    sites = placed(donor_feat[0], rows, 0) + placed(acceptor_feat[0], rows, blk)
    packed = (sites.astype(f32) + whole).astype(bf16)
    base = 0.5 * sum(
        placed(value, BINS + blk, row, lane)
        for value, row, lane in (
            (dist_table, 0, 0),
            (output_weights, BINS, 0),
            (output_weights, BINS + tissues, -width),
        )
    )
    spots = placed(acceptor_pos, BINS + blk, BINS + 2 * tissues)
    spots = spots + placed(acceptor_pos, BINS + blk, BINS + 2 * tissues + 1)
    row = lax.broadcasted_iota(jnp.int32, spots.shape, 0)
    spots = jnp.where(row == BINS + 2 * tissues, spots >> 8, spots & 255)
    base = (base.astype(f32) + spots.astype(f32)).astype(bf16)
    w_in = halved(lax.dynamic_index_in_dim(hidden_weights, lax.axis_index("ctx"), 0, False))
    pieces = [swapped(packed, "ctx", k) for k in GATHER_ORDER]
    tiles = len(tiles_of(blocks))
    chunk = width // (4 * blocks)
    pairs = blk * blk
    partial, loss, grad, slope = pl.pallas_call(
        functools.partial(head_kernel, blocks, blk, width),
        out_shape=(
            jax.ShapeDtypeStruct((2, 2, blocks, chunk, hidden), f32),
            jax.ShapeDtypeStruct((blocks, 8, LANES), f32),
            jax.ShapeDtypeStruct((tiles, pairs, hidden), bf16),
            jax.ShapeDtypeStruct((tiles, pairs, width), f32),
        ),
        scratch_shapes=[
            pltpu.VMEM((BINS + 2 * blocks * blk, width), bf16),
            pltpu.VMEM((blocks * blk, width), bf16),
            pltpu.VMEM((tiles, pairs, BINS), bf16),
            pltpu.VMEM((tiles, pairs, width), bf16),
            pltpu.VMEM((tiles, pairs, hidden), bf16),
            pltpu.VMEM((tiles, pairs, hidden), f32),
            pltpu.VMEM((width, hidden), f32),
        ],
        compiler_params=pltpu.CompilerParams(vmem_limit_bytes=32 * 2**20),
        name="head",
    )(base, w_in, packed, *pieces)
    kept, sent = partial[0], swapped(partial[1], "rep", 1)
    acc = pl.pallas_call(
        functools.partial(acceptor_kernel, blocks, blk),
        out_shape=jax.ShapeDtypeStruct((blocks, blk, width), f32),
        compiler_params=pltpu.CompilerParams(vmem_limit_bytes=16 * 2**20),
        cost_estimate=pl.CostEstimate(
            flops=2 * tiles * pairs * width * hidden,
            bytes_accessed=tiles * pairs * (2 * hidden + 4 * width),
            transcendentals=0,
        ),
        name="acceptors",
    )(grad, w_in, slope)
    partial = kept + sent
    sent = swapped(partial[1].astype(bf16), "rep", 2)
    acc = acc + swapped(acc, "tis", 1)
    partial = partial[0] + sent.astype(jnp.float32)
    cuts = [part[:, :, i : i + LANES] for part in (partial, acc) for i in range(0, part.shape[2], LANES)]
    send = jnp.concatenate(cuts + [loss], axis=1)
    arrived = [send[0]] + [swapped(send[k], "ctx", k) for k in RETURN_ORDER]
    donor_loss, grad_hidden, grad_acceptor = pl.pallas_call(
        functools.partial(finish_kernel, blocks, width, hidden),
        out_shape=(
            jax.ShapeDtypeStruct((1, tissues, blk), jnp.float32),
            jax.ShapeDtypeStruct((tissues, chunk, hidden), jnp.float32),
            jax.ShapeDtypeStruct((1, blk, width), jnp.float32),
        ),
        compiler_params=pltpu.CompilerParams(vmem_limit_bytes=8 * 2**20),
        name="finish",
    )(*arrived)
    return (jnp.transpose(donor_loss, (0, 2, 1)), grad_hidden, grad_acceptor)


def on_device(*args):
    donor_feat, acceptor_feat, _, _, pair_mask, _, _, hidden_weights, _ = args
    blocks = lax.axis_size("ctx")
    tissues, width, hidden = hidden_weights.shape
    blk = donor_feat.shape[1]
    fits = (
        donor_feat.shape[0] == 1
        and tissues == blocks == 4
        and lax.axis_size("rep") == 4
        and lax.axis_size("tis") == 2
        and acceptor_feat.shape[1] == blk == 16
        and width == 256
        and hidden == 2 * width
        and pair_mask.shape[2] == (SPAN_BLOCKS + 1) * blk
        and BINS == LANES == 2 * blocks * blk
    )
    return shared(*args) if fits else general(*args)


def solution(mesh):
    placed = (
        P("rep", "ctx", None),
        P("rep", "ctx", None),
        P("rep", "ctx"),
        P("rep", None),
        P("rep", "ctx", None),
        P("rep", "ctx", "tis"),
        P(),
        P("tis", None, None),
        P("tis", None),
    )
    return jax.shard_map(
        on_device,
        mesh=mesh,
        in_specs=placed,
        out_specs=(P("rep", "ctx", "tis"), P("tis", ("ctx", "rep"), None), P("rep", "ctx", None)),
        check_vma=False,
    )
```

```python
import functools

import jax
import jax.numpy as jnp
from jax import lax
from jax.experimental import pallas as pl
from jax.experimental.pallas import tpu as pltpu
from jax.sharding import PartitionSpec as P

BLOCK_BP = 65536
SPAN_BLOCKS = 4
BIN_BP = 2048
BINS = 128
LANES = 128
GATHER_ORDER = (1, 3, 2)
RETURN_ORDER = (1, 3, 2)
LAGS = (10, 12, 13)


def passed_along(value, axis, steps):
    count = lax.axis_size(axis)
    first, last = (max(0, -steps), min(count, count - steps))
    return lax.ppermute(value, axis, [(source, source + steps) for source in range(first, last)])


def swapped(value, axis, bits):
    return lax.ppermute(value, axis, [(i, i ^ bits) for i in range(lax.axis_size(axis))])


def silu_grad(values):
    sig = jax.nn.sigmoid(values)
    return sig * (1.0 + values * (1.0 - sig))


def general(
    donor_feat,
    acceptor_feat,
    donor_pos,
    acceptor_pos,
    pair_mask,
    targets,
    dist_table,
    hidden_weights,
    output_weights,
):
    seq_dev, don_blk, width = donor_feat.shape
    acc_blk = acceptor_feat.shape[1]
    blocks = lax.axis_size("ctx")
    reach = SPAN_BLOCKS + 1
    slots = reach * acc_blk
    here = lax.axis_index("ctx")
    pieces = [acceptor_feat]
    for offset in range(1, reach):
        pieces.append(
            passed_along(acceptor_feat, "ctx", -offset)
            if offset < blocks
            else jnp.zeros_like(acceptor_feat)
        )
    window = jnp.stack(pieces, axis=1).reshape(seq_dev, slots, width)
    pos_pad = jnp.concatenate(
        [acceptor_pos, jnp.zeros((seq_dev, SPAN_BLOCKS * acc_blk), jnp.int32)], axis=1
    )
    pos_win = lax.dynamic_slice_in_dim(pos_pad, here * acc_blk, slots, 1)
    slot_block = jnp.arange(slots, dtype=jnp.int32) // acc_blk
    inchain = here + slot_block < blocks
    dist = slot_block * BLOCK_BP + pos_win[:, None, :] - donor_pos[:, :, None]
    valid = (pair_mask > 0) & (dist > 0) & (dist <= SPAN_BLOCKS * BLOCK_BP) & inchain[None, None, :]
    bins = jnp.clip((dist - 1) // BIN_BP, 0, BINS - 1)
    lookup = (
        (bins[..., None] == jnp.arange(BINS, dtype=jnp.int32))
        .astype(jnp.bfloat16)
        .reshape(-1, BINS)
    )
    table = jnp.dot(lookup, dist_table, preferred_element_type=jnp.float32).reshape(
        seq_dev, don_blk, slots, width
    )
    pre = (
        donor_feat.astype(jnp.float32)[:, :, None, :] + window.astype(jnp.float32)[:, None] + table
    )
    flat = jax.nn.silu(pre).astype(jnp.bfloat16).reshape(-1, width)
    grad_pair = jnp.zeros((flat.shape[0], width), jnp.float32)
    losses = []
    fulls = []
    slot_ids = jnp.arange(slots, dtype=jnp.int32)
    for tissue in range(hidden_weights.shape[0]):
        w_in = hidden_weights[tissue]
        w_out = output_weights[tissue]
        goal = targets[:, :, tissue]
        hid = jnp.dot(flat, w_in, preferred_element_type=jnp.float32)
        act = jax.nn.silu(hid).astype(jnp.bfloat16)
        logits = jnp.dot(act, w_out, preferred_element_type=jnp.float32).reshape(
            seq_dev, don_blk, slots
        )
        masked = jnp.where(valid, logits, -jnp.inf)
        top = jnp.maximum(jnp.max(masked, axis=-1), 0.0)
        expo = jnp.exp(masked - top[..., None])
        total = jnp.sum(expo, axis=-1) + jnp.exp(-top)
        onehot = goal[..., None] == slot_ids
        picked = jnp.sum(jnp.where(onehot, logits, 0.0), axis=-1)
        losses.append(top + jnp.log(total) - picked)
        grad_logits = expo / total[..., None] - onehot.astype(jnp.float32)
        grad_act = grad_logits.reshape(-1)[:, None] * w_out.astype(jnp.float32)[None, :]
        grad_hid = (grad_act * silu_grad(hid)).astype(jnp.bfloat16)
        grad_pair = grad_pair + lax.dot_general(
            grad_hid, w_in, (((1,), (1,)), ((), ())), preferred_element_type=jnp.float32
        )
        fulls.append(
            lax.dot_general(
                flat, grad_hid, (((0,), (0,)), ((), ())), preferred_element_type=jnp.float32
            )
        )
    stacked = jnp.stack(fulls, axis=1)
    grad_hidden = jnp.transpose(
        lax.psum_scatter(stacked, ("ctx", "rep"), scatter_dimension=0, tiled=True), (1, 0, 2)
    )
    grad_pre = grad_pair.reshape(seq_dev, don_blk, slots, width) * silu_grad(pre)
    contrib = jnp.sum(grad_pre, axis=1).reshape(seq_dev, reach, acc_blk, width)
    carried = contrib[:, 0]
    for offset in range(1, min(reach, blocks)):
        carried = carried + passed_along(contrib[:, offset], "ctx", offset)
    grad_acceptor = lax.psum(carried, "tis")
    donor_loss = jnp.stack(losses, axis=-1)
    return (donor_loss, grad_hidden, grad_acceptor)


def halved(value):
    return (value.astype(jnp.float32) * 0.5).astype(value.dtype)


def silu_parts(half):
    turn = jnp.tanh(half)
    value = half + half * turn
    return value, 2.0 - (1.0 - value) * (1.0 - turn)


def ones_dot(left, right):
    return jnp.dot(left, right, preferred_element_type=jnp.float32)


def tiles_of(blocks):
    return [(b, a) for b in range(blocks) for a in range(b, min(blocks, b + SPAN_BLOCKS + 1))]


def head_kernel(blocks, blk, width, *refs):
    (base_ref, w_ref) = refs[:2]
    packed = refs[2 : blocks + 2]
    (gh_ref, send_ref, loss_ref, grad_s, dpre_s) = refs[blocks + 2 : blocks + 7]
    (source, aux, picks_s, pair_s, act_s, dhid_s) = refs[blocks + 7 :]
    here = lax.axis_index("ctx")
    rep = lax.axis_index("rep")
    cross = lax.div(rep, 2)
    core = lax.rem(rep, 2)
    f32, bf16 = jnp.float32, jnp.bfloat16
    hidden = gh_ref.shape[1]
    pairs = blk * blk
    sites = blocks * blk
    slots = (SPAN_BLOCKS + 1) * blk
    tiles = tiles_of(blocks)

    source[:BINS, :] = base_ref[:BINS, :]
    for piece, k in zip(packed, (0,) + GATHER_ORDER):
        start = pl.multiple_of((here ^ k) * blk, blk)
        source[pl.ds(BINS + start, blk), :] = halved(piece[:blk, :])
        source[pl.ds(BINS + sites + start, blk), :] = halved(piece[blk : 2 * blk, :])
        aux[pl.ds(start, blk), :] = piece[2 * blk :, :]

    lanes = lax.broadcasted_iota(jnp.int32, (blk, LANES), 1)
    ids = lax.broadcasted_iota(jnp.int32, (blk, LANES), 0)
    spots = base_ref[BINS:, :LANES].astype(f32)
    apos = spots[2 * blocks : 2 * blocks + 1, :] * 256.0
    apos = apos + spots[2 * blocks + 1 : 2 * blocks + 2, :]
    codes = []
    aims = []
    for b in range(blocks):
        extra = aux[b * blk : (b + 1) * blk, :].astype(f32)
        rows = extra[:, LANES:]

        def column(row):
            return jnp.sum(jnp.where(lanes == ids, row, 0.0), axis=1, keepdims=True)

        dpos = column(rows[:1, :] * 256.0 + rows[1:2, :])
        aim = column(
            jnp.sum(jnp.where(ids == here + 4, rows, 0.0), axis=0, keepdims=True)
        ).astype(jnp.int32)
        mask = pltpu.roll(extra[:, :LANES], b * blk, 1) if b else extra[:, :LANES]
        dist = (lanes // blk - b) * BLOCK_BP + (apos - dpos).astype(jnp.int32)
        valid = (mask > 0.5) & (dist > 0) & (dist <= SPAN_BLOCKS * BLOCK_BP) & (lanes < sites)
        code = jnp.where(valid, jnp.clip((dist - 1) // BIN_BP, 0, BINS - 1), -1)
        codes.append(code.astype(f32))
        aims.append(jnp.where(aim == slots, -1, aim + b * blk))

    w_half = w_ref[...]
    w_out = base_ref[BINS:, :].astype(f32)
    tissues = blocks
    row_ids = lax.broadcasted_iota(jnp.int32, w_out.shape, 0)
    w_out = jnp.concatenate(
        [
            jnp.sum(jnp.where(row_ids == here + part * tissues, w_out, 0.0), axis=0, keepdims=True)
            for part in range(hidden // width)
        ],
        axis=1,
    )
    w_rows = jnp.broadcast_to(w_out * 2.0, (LANES, hidden)).astype(bf16)
    ones = jnp.ones((LANES, LANES), bf16)
    lane3 = lax.broadcasted_iota(jnp.int32, (blk, blk, LANES), 2)
    row3 = lax.broadcasted_iota(jnp.int32, (blk, blk, LANES), 1)
    don3 = lax.broadcasted_iota(jnp.int32, (blk, blk, LANES), 0)
    lane_f = lax.broadcasted_iota(jnp.int32, (pairs, LANES), 1).astype(f32)
    from_donor = [
        jnp.where(lane3 == don3 + b * blk, 1.0, 0.0).astype(bf16).reshape(pairs, LANES)
        for b in range(blocks)
    ]
    from_acceptor = [
        jnp.where(lane3 == row3 + (sites + a * blk), 1.0, 0.0).astype(bf16).reshape(pairs, LANES)
        for a in range(blocks)
    ]
    slot_of = [lane3 == row3 + a * blk for a in range(blocks)]
    twice_of = [pick | (lane3 == row3 + (sites + a * blk)) for a, pick in enumerate(slot_of)]
    spread_out = [jnp.zeros((blk, blk, LANES), f32)] * blocks

    def bins_of(tile):
        b, a = tiles[tile]
        code = jnp.where(slot_of[a], codes[b][:, None, :], 0.0).astype(bf16)
        code = ones_dot(code.reshape(pairs, LANES), ones)
        picks_s[tile] = jnp.where(code == lane_f, 1.0, 0.0).astype(bf16)

    def pair_of(tile):
        b, a = tiles[tile]
        picks = jnp.concatenate([picks_s[tile], from_donor[b] + from_acceptor[a]], axis=1)
        value, slope = silu_parts(ones_dot(picks, source[...]))
        pair_s[tile] = value.astype(bf16)
        dpre_s[tile] = slope

    def hidden_of(tile):
        value, slope = silu_parts(ones_dot(pair_s[tile], w_half))
        act_s[tile] = value.astype(bf16)
        dhid_s[tile] = slope * w_out

    def logits_of(tile):
        b, a = tiles[tile]
        logit = lax.dot_general(
            act_s[tile], w_rows, (((1,), (1,)), ((), ())), preferred_element_type=f32
        )
        spread_out[b] = jnp.where(slot_of[a], logit.reshape(blk, blk, LANES), spread_out[b])

    stages = [(bins_of, 0), (pair_of, LAGS[0]), (hidden_of, LAGS[1]), (logits_of, LAGS[2])]
    for step in range(len(tiles) + stages[-1][1]):
        for stage, lag in stages:
            if 0 <= step - lag < len(tiles):
                stage(step - lag)
    grads = []
    for b in range(blocks):
        logit = jnp.sum(spread_out[b], axis=1)
        chosen = lanes == aims[b]
        masked = jnp.where(codes[b] >= 0.0, logit, -jnp.inf)
        top = jnp.maximum(jnp.max(masked, axis=1, keepdims=True), 0.0)
        expo = jnp.exp(masked - top)
        total = jnp.sum(expo, axis=1, keepdims=True) + jnp.exp(-top)
        picked = jnp.sum(jnp.where(chosen, logit, 0.0), axis=1, keepdims=True)
        loss = jnp.where(lanes == ids, top + jnp.log(total) - picked, 0.0)
        loss = jnp.sum(loss, axis=0, keepdims=True)
        loss_ref[b ^ here] = jnp.broadcast_to(loss, loss_ref.shape[1:])
        grad = expo / total - jnp.where(chosen, 1.0, 0.0)
        high = grad.astype(bf16).astype(f32)
        grads.append(high + pltpu.roll(grad - high, sites, 1))
    def gradient_of(start, stop):
        count = (stop - start) * pairs
        return lax.dot_general(
            pair_s[start:stop].reshape(count, width),
            grad_s[start:stop].reshape(count, hidden),
            (((0,), (0,)), ((), ())),
            preferred_element_type=f32,
        )

    middle = len(tiles) // 2
    for tile, (b, a) in enumerate(tiles):
        rows = jnp.where(twice_of[a], grads[b][:, None, :], 0.0).astype(bf16)
        rows = ones_dot(rows.reshape(pairs, LANES), ones)
        rows = jnp.concatenate([rows] * (hidden // LANES), axis=1)
        grad_s[tile] = (rows * dhid_s[tile]).astype(bf16)
        if tile == middle:
            gh_ref[...] = gradient_of(0, middle)
    gh_ref[...] += gradient_of(middle, len(tiles))
    chunk = send_ref.shape[2]
    for x in range(2):
        for c in range(blocks):
            start = (((c ^ here) * 2 + (x ^ cross)) * 2 + 1 - core) * chunk
            send_ref[x, c] = gh_ref[pl.ds(pl.multiple_of(start, chunk), chunk), :]


def core_kernel(blocks, gh_ref, sent_ref, kept_ref, send_ref):
    here = lax.axis_index("ctx")
    rep = lax.axis_index("rep")
    cross = lax.div(rep, 2)
    core = lax.rem(rep, 2)
    chunk = sent_ref.shape[2]
    for x in range(2):
        for c in range(blocks):
            start = (((c ^ here) * 2 + (x ^ cross)) * 2 + core) * chunk
            rows = gh_ref[pl.ds(pl.multiple_of(start, chunk), chunk), :] + sent_ref[x, c]
            if x:
                send_ref[c] = rows.astype(send_ref.dtype)
            else:
                kept_ref[c] = rows


def finish_kernel(parts, width, hidden, *refs):
    pieces = refs[:parts]
    (loss_ref, gh_ref, acc_ref) = refs[parts:]
    here = lax.axis_index("ctx")
    blk = acc_ref.shape[1]
    total = None
    for piece, k in zip(pieces, (0,) + RETURN_ORDER):
        owner = here ^ k
        groups = (hidden + width) // LANES
        cuts = [piece[i * blk : (i + 1) * blk, :] for i in range(groups)]
        gh_ref[owner] = jnp.concatenate(cuts[: hidden // LANES], axis=1)
        acc = jnp.concatenate(cuts[hidden // LANES :], axis=1)
        total = acc if total is None else total + acc
        loss_ref[0, pl.ds(owner, 1), :] = piece[groups * blk : groups * blk + 1, :blk]
    acc_ref[0] = total


def acceptor_kernel(blocks, blk, grad_ref, w_ref, slope_ref, out_ref):
    here = lax.axis_index("ctx")
    w = w_ref[...]
    width = w.shape[0]
    total = [None] * blocks
    for tile, (_, a) in enumerate(tiles_of(blocks)):
        grad_pair = lax.dot_general(
            grad_ref[tile], w, (((1,), (1,)), ((), ())), preferred_element_type=jnp.float32
        )
        part = jnp.sum((grad_pair * slope_ref[tile]).reshape(blk, blk, width), axis=0)
        total[a] = part if total[a] is None else total[a] + part
    for a in range(blocks):
        out_ref[a ^ here] = total[a]


def shared(
    donor_feat,
    acceptor_feat,
    donor_pos,
    acceptor_pos,
    pair_mask,
    targets,
    dist_table,
    hidden_weights,
    output_weights,
):
    _, blk, width = donor_feat.shape
    blocks = lax.axis_size("ctx")
    tissues, _, hidden = hidden_weights.shape
    bf16 = jnp.bfloat16
    f32 = jnp.float32
    def placed(value, rows, row, lane=0):
        height, extent = value.shape
        room = ((row, rows - row - height, 0), (lane, width - lane - extent, 0))
        return lax.pad(value, jnp.zeros((), value.dtype), room)

    rows = 3 * blk
    last = 2 * blk
    whole = sum(
        placed(value, rows, row, lane)
        for value, row, lane in (
            (pair_mask[0], last, 0),
            (donor_pos, last, LANES),
            (donor_pos, last + 1, LANES),
            (jnp.transpose(targets, (0, 2, 1))[0], last + 4, LANES),
        )
    )
    row = lax.broadcasted_iota(jnp.int32, whole.shape, 0)
    lane = lax.broadcasted_iota(jnp.int32, whole.shape, 1)
    whole = jnp.where((lane >= LANES) & (row == last), whole >> 8, whole & 255).astype(f32)
    sites = placed(donor_feat[0], rows, 0) + placed(acceptor_feat[0], rows, blk)
    packed = (sites.astype(f32) + whole).astype(bf16)
    base = 0.5 * sum(
        placed(value, BINS + blk, row, lane)
        for value, row, lane in (
            (dist_table, 0, 0),
            (output_weights, BINS, 0),
            (output_weights, BINS + tissues, -width),
        )
    )
    spots = placed(acceptor_pos, BINS + blk, BINS + 2 * tissues)
    spots = spots + placed(acceptor_pos, BINS + blk, BINS + 2 * tissues + 1)
    row = lax.broadcasted_iota(jnp.int32, spots.shape, 0)
    spots = jnp.where(row == BINS + 2 * tissues, spots >> 8, spots & 255)
    base = (base.astype(f32) + spots.astype(f32)).astype(bf16)
    w_in = halved(lax.dynamic_index_in_dim(hidden_weights, lax.axis_index("ctx"), 0, False))
    pieces = [swapped(packed, "ctx", k) for k in GATHER_ORDER]
    tiles = len(tiles_of(blocks))
    chunk = width // (4 * blocks)
    pairs = blk * blk
    partial, sent, loss, grad, slope = pl.pallas_call(
        functools.partial(head_kernel, blocks, blk, width),
        out_shape=(
            jax.ShapeDtypeStruct((width, hidden), f32),
            jax.ShapeDtypeStruct((2, blocks, chunk, hidden), f32),
            jax.ShapeDtypeStruct((blocks, 8, LANES), f32),
            jax.ShapeDtypeStruct((tiles, pairs, hidden), bf16),
            jax.ShapeDtypeStruct((tiles, pairs, width), f32),
        ),
        scratch_shapes=[
            pltpu.VMEM((BINS + 2 * blocks * blk, width), bf16),
            pltpu.VMEM((blocks * blk, width), bf16),
            pltpu.VMEM((tiles, pairs, BINS), bf16),
            pltpu.VMEM((tiles, pairs, width), bf16),
            pltpu.VMEM((tiles, pairs, hidden), bf16),
            pltpu.VMEM((tiles, pairs, hidden), f32),
        ],
        compiler_params=pltpu.CompilerParams(vmem_limit_bytes=32 * 2**20),
        name="head",
    )(base, w_in, packed, *pieces)
    sent = swapped(sent, "rep", 1)
    acc = pl.pallas_call(
        functools.partial(acceptor_kernel, blocks, blk),
        out_shape=jax.ShapeDtypeStruct((blocks, blk, width), f32),
        compiler_params=pltpu.CompilerParams(vmem_limit_bytes=16 * 2**20),
        cost_estimate=pl.CostEstimate(
            flops=2 * tiles * pairs * width * hidden,
            bytes_accessed=tiles * pairs * (2 * hidden + 4 * width),
            transcendentals=0,
        ),
        name="acceptors",
    )(grad, w_in, slope)
    kept, sent = pl.pallas_call(
        functools.partial(core_kernel, blocks),
        out_shape=(
            jax.ShapeDtypeStruct((blocks, chunk, hidden), f32),
            jax.ShapeDtypeStruct((blocks, chunk, hidden), bf16),
        ),
        compiler_params=pltpu.CompilerParams(vmem_limit_bytes=8 * 2**20),
        name="core",
    )(partial, sent)
    sent = swapped(sent, "rep", 2)
    acc = acc + swapped(acc, "tis", 1)
    partial = kept + sent.astype(f32)
    cuts = [part[:, :, i : i + LANES] for part in (partial, acc) for i in range(0, part.shape[2], LANES)]
    send = jnp.concatenate(cuts + [loss], axis=1)
    arrived = [send[0]] + [swapped(send[k], "ctx", k) for k in RETURN_ORDER]
    donor_loss, grad_hidden, grad_acceptor = pl.pallas_call(
        functools.partial(finish_kernel, blocks, width, hidden),
        out_shape=(
            jax.ShapeDtypeStruct((1, tissues, blk), jnp.float32),
            jax.ShapeDtypeStruct((tissues, chunk, hidden), jnp.float32),
            jax.ShapeDtypeStruct((1, blk, width), jnp.float32),
        ),
        compiler_params=pltpu.CompilerParams(vmem_limit_bytes=8 * 2**20),
        name="finish",
    )(*arrived)
    return (jnp.transpose(donor_loss, (0, 2, 1)), grad_hidden, grad_acceptor)


def on_device(*args):
    donor_feat, acceptor_feat, _, _, pair_mask, _, _, hidden_weights, _ = args
    blocks = lax.axis_size("ctx")
    tissues, width, hidden = hidden_weights.shape
    blk = donor_feat.shape[1]
    fits = (
        donor_feat.shape[0] == 1
        and tissues == blocks == 4
        and lax.axis_size("rep") == 4
        and lax.axis_size("tis") == 2
        and acceptor_feat.shape[1] == blk == 16
        and width == 256
        and hidden == 2 * width
        and pair_mask.shape[2] == (SPAN_BLOCKS + 1) * blk
        and BINS == LANES == 2 * blocks * blk
    )
    return shared(*args) if fits else general(*args)


def solution(mesh):
    placed = (
        P("rep", "ctx", None),
        P("rep", "ctx", None),
        P("rep", "ctx"),
        P("rep", None),
        P("rep", "ctx", None),
        P("rep", "ctx", "tis"),
        P(),
        P("tis", None, None),
        P("tis", None),
    )
    return jax.shard_map(
        on_device,
        mesh=mesh,
        in_specs=placed,
        out_specs=(P("rep", "ctx", "tis"), P("tis", ("ctx", "rep"), None), P("rep", "ctx", None)),
        check_vma=False,
    )
```

```python
import functools

import jax
import jax.numpy as jnp
from jax import lax
from jax.experimental import pallas as pl
from jax.experimental.pallas import tpu as pltpu
from jax.sharding import PartitionSpec as P

BLOCK_BP = 65536
SPAN_BLOCKS = 4
BIN_BP = 2048
BINS = 128
LANES = 128
GATHER_ORDER = (1, 3, 2)
RETURN_ORDER = (1, 3, 2)
LAGS = (10, 12, 13)


def passed_along(value, axis, steps):
    count = lax.axis_size(axis)
    first, last = (max(0, -steps), min(count, count - steps))
    return lax.ppermute(value, axis, [(source, source + steps) for source in range(first, last)])


def swapped(value, axis, bits):
    return lax.ppermute(value, axis, [(i, i ^ bits) for i in range(lax.axis_size(axis))])


def silu_grad(values):
    sig = jax.nn.sigmoid(values)
    return sig * (1.0 + values * (1.0 - sig))


def general(
    donor_feat,
    acceptor_feat,
    donor_pos,
    acceptor_pos,
    pair_mask,
    targets,
    dist_table,
    hidden_weights,
    output_weights,
):
    seq_dev, don_blk, width = donor_feat.shape
    acc_blk = acceptor_feat.shape[1]
    blocks = lax.axis_size("ctx")
    reach = SPAN_BLOCKS + 1
    slots = reach * acc_blk
    here = lax.axis_index("ctx")
    pieces = [acceptor_feat]
    for offset in range(1, reach):
        pieces.append(
            passed_along(acceptor_feat, "ctx", -offset)
            if offset < blocks
            else jnp.zeros_like(acceptor_feat)
        )
    window = jnp.stack(pieces, axis=1).reshape(seq_dev, slots, width)
    pos_pad = jnp.concatenate(
        [acceptor_pos, jnp.zeros((seq_dev, SPAN_BLOCKS * acc_blk), jnp.int32)], axis=1
    )
    pos_win = lax.dynamic_slice_in_dim(pos_pad, here * acc_blk, slots, 1)
    slot_block = jnp.arange(slots, dtype=jnp.int32) // acc_blk
    inchain = here + slot_block < blocks
    dist = slot_block * BLOCK_BP + pos_win[:, None, :] - donor_pos[:, :, None]
    valid = (pair_mask > 0) & (dist > 0) & (dist <= SPAN_BLOCKS * BLOCK_BP) & inchain[None, None, :]
    bins = jnp.clip((dist - 1) // BIN_BP, 0, BINS - 1)
    lookup = (
        (bins[..., None] == jnp.arange(BINS, dtype=jnp.int32))
        .astype(jnp.bfloat16)
        .reshape(-1, BINS)
    )
    table = jnp.dot(lookup, dist_table, preferred_element_type=jnp.float32).reshape(
        seq_dev, don_blk, slots, width
    )
    pre = (
        donor_feat.astype(jnp.float32)[:, :, None, :] + window.astype(jnp.float32)[:, None] + table
    )
    flat = jax.nn.silu(pre).astype(jnp.bfloat16).reshape(-1, width)
    grad_pair = jnp.zeros((flat.shape[0], width), jnp.float32)
    losses = []
    fulls = []
    slot_ids = jnp.arange(slots, dtype=jnp.int32)
    for tissue in range(hidden_weights.shape[0]):
        w_in = hidden_weights[tissue]
        w_out = output_weights[tissue]
        goal = targets[:, :, tissue]
        hid = jnp.dot(flat, w_in, preferred_element_type=jnp.float32)
        act = jax.nn.silu(hid).astype(jnp.bfloat16)
        logits = jnp.dot(act, w_out, preferred_element_type=jnp.float32).reshape(
            seq_dev, don_blk, slots
        )
        masked = jnp.where(valid, logits, -jnp.inf)
        top = jnp.maximum(jnp.max(masked, axis=-1), 0.0)
        expo = jnp.exp(masked - top[..., None])
        total = jnp.sum(expo, axis=-1) + jnp.exp(-top)
        onehot = goal[..., None] == slot_ids
        picked = jnp.sum(jnp.where(onehot, logits, 0.0), axis=-1)
        losses.append(top + jnp.log(total) - picked)
        grad_logits = expo / total[..., None] - onehot.astype(jnp.float32)
        grad_act = grad_logits.reshape(-1)[:, None] * w_out.astype(jnp.float32)[None, :]
        grad_hid = (grad_act * silu_grad(hid)).astype(jnp.bfloat16)
        grad_pair = grad_pair + lax.dot_general(
            grad_hid, w_in, (((1,), (1,)), ((), ())), preferred_element_type=jnp.float32
        )
        fulls.append(
            lax.dot_general(
                flat, grad_hid, (((0,), (0,)), ((), ())), preferred_element_type=jnp.float32
            )
        )
    stacked = jnp.stack(fulls, axis=1)
    grad_hidden = jnp.transpose(
        lax.psum_scatter(stacked, ("ctx", "rep"), scatter_dimension=0, tiled=True), (1, 0, 2)
    )
    grad_pre = grad_pair.reshape(seq_dev, don_blk, slots, width) * silu_grad(pre)
    contrib = jnp.sum(grad_pre, axis=1).reshape(seq_dev, reach, acc_blk, width)
    carried = contrib[:, 0]
    for offset in range(1, min(reach, blocks)):
        carried = carried + passed_along(contrib[:, offset], "ctx", offset)
    grad_acceptor = lax.psum(carried, "tis")
    donor_loss = jnp.stack(losses, axis=-1)
    return (donor_loss, grad_hidden, grad_acceptor)


def halved(value):
    return (value.astype(jnp.float32) * 0.5).astype(value.dtype)


def silu_parts(half):
    turn = jnp.tanh(half)
    value = half + half * turn
    return value, 2.0 - (1.0 - value) * (1.0 - turn)


def ones_dot(left, right):
    return jnp.dot(left, right, preferred_element_type=jnp.float32)


def tiles_of(blocks):
    return [(b, a) for b in range(blocks) for a in range(b, min(blocks, b + SPAN_BLOCKS + 1))]


def head_kernel(blocks, blk, width, *refs):
    (base_ref, w_ref) = refs[:2]
    packed = refs[2 : blocks + 2]
    (gh_ref, send_ref, loss_ref, grad_s, dpre_s) = refs[blocks + 2 : blocks + 7]
    (source, aux, picks_s, pair_s, act_s, dhid_s) = refs[blocks + 7 :]
    here = lax.axis_index("ctx")
    rep = lax.axis_index("rep")
    cross = lax.div(rep, 2)
    core = lax.rem(rep, 2)
    f32, bf16 = jnp.float32, jnp.bfloat16
    hidden = gh_ref.shape[1]
    pairs = blk * blk
    sites = blocks * blk
    slots = (SPAN_BLOCKS + 1) * blk
    tiles = tiles_of(blocks)

    source[:BINS, :] = base_ref[:BINS, :]
    for piece, k in zip(packed, (0,) + GATHER_ORDER):
        start = pl.multiple_of((here ^ k) * blk, blk)
        source[pl.ds(BINS + start, blk), :] = halved(piece[:blk, :])
        source[pl.ds(BINS + sites + start, blk), :] = halved(piece[blk : 2 * blk, :])
        aux[pl.ds(start, blk), :] = piece[2 * blk :, :]

    lanes = lax.broadcasted_iota(jnp.int32, (blk, LANES), 1)
    ids = lax.broadcasted_iota(jnp.int32, (blk, LANES), 0)
    spots = base_ref[BINS:, :LANES].astype(f32)
    apos = spots[2 * blocks : 2 * blocks + 1, :] * 256.0
    apos = apos + spots[2 * blocks + 1 : 2 * blocks + 2, :]
    codes = []
    aims = []
    for b in range(blocks):
        extra = aux[b * blk : (b + 1) * blk, :].astype(f32)
        rows = extra[:, LANES:]

        def column(row):
            return jnp.sum(jnp.where(lanes == ids, row, 0.0), axis=1, keepdims=True)

        dpos = column(rows[:1, :] * 256.0 + rows[1:2, :])
        aim = column(
            jnp.sum(jnp.where(ids == here + 4, rows, 0.0), axis=0, keepdims=True)
        ).astype(jnp.int32)
        mask = pltpu.roll(extra[:, :LANES], b * blk, 1) if b else extra[:, :LANES]
        dist = (lanes // blk - b) * BLOCK_BP + (apos - dpos).astype(jnp.int32)
        valid = (mask > 0.5) & (dist > 0) & (dist <= SPAN_BLOCKS * BLOCK_BP) & (lanes < sites)
        code = jnp.where(valid, jnp.clip((dist - 1) // BIN_BP, 0, BINS - 1), -1)
        codes.append(code.astype(f32))
        aims.append(jnp.where(aim == slots, -1, aim + b * blk))

    w_half = w_ref[...]
    w_out = base_ref[BINS:, :].astype(f32)
    tissues = blocks
    row_ids = lax.broadcasted_iota(jnp.int32, w_out.shape, 0)
    w_out = jnp.concatenate(
        [
            jnp.sum(jnp.where(row_ids == here + part * tissues, w_out, 0.0), axis=0, keepdims=True)
            for part in range(hidden // width)
        ],
        axis=1,
    )
    w_rows = jnp.broadcast_to(w_out * 2.0, (LANES, hidden)).astype(bf16)
    ones = jnp.ones((LANES, LANES), bf16)
    lane3 = lax.broadcasted_iota(jnp.int32, (blk, blk, LANES), 2)
    row3 = lax.broadcasted_iota(jnp.int32, (blk, blk, LANES), 1)
    don3 = lax.broadcasted_iota(jnp.int32, (blk, blk, LANES), 0)
    lane_f = lax.broadcasted_iota(jnp.int32, (pairs, LANES), 1).astype(f32)
    from_donor = [
        jnp.where(lane3 == don3 + b * blk, 1.0, 0.0).astype(bf16).reshape(pairs, LANES)
        for b in range(blocks)
    ]
    from_acceptor = [
        jnp.where(lane3 == row3 + (sites + a * blk), 1.0, 0.0).astype(bf16).reshape(pairs, LANES)
        for a in range(blocks)
    ]
    slot_of = [lane3 == row3 + a * blk for a in range(blocks)]
    twice_of = [pick | (lane3 == row3 + (sites + a * blk)) for a, pick in enumerate(slot_of)]
    spread_out = [jnp.zeros((blk, blk, LANES), f32)] * blocks

    def bins_of(tile):
        b, a = tiles[tile]
        code = jnp.where(slot_of[a], codes[b][:, None, :], 0.0).astype(bf16)
        code = ones_dot(code.reshape(pairs, LANES), ones)
        picks_s[tile] = jnp.where(code == lane_f, 1.0, 0.0).astype(bf16)

    def pair_of(tile):
        b, a = tiles[tile]
        picks = jnp.concatenate([picks_s[tile], from_donor[b] + from_acceptor[a]], axis=1)
        value, slope = silu_parts(ones_dot(picks, source[...]))
        pair_s[tile] = value.astype(bf16)
        dpre_s[tile] = slope

    def hidden_of(tile):
        value, slope = silu_parts(ones_dot(pair_s[tile], w_half))
        act_s[tile] = value.astype(bf16)
        dhid_s[tile] = slope * w_out

    def logits_of(tile):
        b, a = tiles[tile]
        logit = lax.dot_general(
            act_s[tile], w_rows, (((1,), (1,)), ((), ())), preferred_element_type=f32
        )
        spread_out[b] = jnp.where(slot_of[a], logit.reshape(blk, blk, LANES), spread_out[b])

    stages = [(bins_of, 0), (pair_of, LAGS[0]), (hidden_of, LAGS[1]), (logits_of, LAGS[2])]
    for step in range(len(tiles) + stages[-1][1]):
        for stage, lag in stages:
            if 0 <= step - lag < len(tiles):
                stage(step - lag)
    grads = []
    for b in range(blocks):
        logit = jnp.sum(spread_out[b], axis=1)
        chosen = lanes == aims[b]
        masked = jnp.where(codes[b] >= 0.0, logit, -jnp.inf)
        top = jnp.maximum(jnp.max(masked, axis=1, keepdims=True), 0.0)
        expo = jnp.exp(masked - top)
        total = jnp.sum(expo, axis=1, keepdims=True) + jnp.exp(-top)
        picked = jnp.sum(jnp.where(chosen, logit, 0.0), axis=1, keepdims=True)
        loss = jnp.where(lanes == ids, top + jnp.log(total) - picked, 0.0)
        loss = jnp.sum(loss, axis=0, keepdims=True)
        loss_ref[b ^ here] = jnp.broadcast_to(loss, loss_ref.shape[1:])
        grad = expo / total - jnp.where(chosen, 1.0, 0.0)
        high = grad.astype(bf16).astype(f32)
        grads.append(high + pltpu.roll(grad - high, sites, 1))
    def gradient_of(start, stop):
        count = (stop - start) * pairs
        return lax.dot_general(
            pair_s[start:stop].reshape(count, width),
            grad_s[start:stop].reshape(count, hidden),
            (((0,), (0,)), ((), ())),
            preferred_element_type=f32,
        )

    middle = 7 * len(tiles) // 10
    for tile, (b, a) in enumerate(tiles):
        rows = jnp.where(twice_of[a], grads[b][:, None, :], 0.0).astype(bf16)
        rows = ones_dot(rows.reshape(pairs, LANES), ones)
        rows = jnp.concatenate([rows] * (hidden // LANES), axis=1)
        grad_s[tile] = (rows * dhid_s[tile]).astype(bf16)
        if tile == middle:
            gh_ref[...] = gradient_of(0, middle)
    gh_ref[...] += gradient_of(middle, len(tiles))
    chunk = send_ref.shape[2]
    for x in range(2):
        for c in range(blocks):
            start = (((c ^ here) * 2 + (x ^ cross)) * 2 + 1 - core) * chunk
            send_ref[x, c] = gh_ref[pl.ds(pl.multiple_of(start, chunk), chunk), :]


def core_kernel(blocks, gh_ref, sent_ref, kept_ref, send_ref):
    here = lax.axis_index("ctx")
    rep = lax.axis_index("rep")
    cross = lax.div(rep, 2)
    core = lax.rem(rep, 2)
    chunk = sent_ref.shape[2]
    for x in range(2):
        for c in range(blocks):
            start = (((c ^ here) * 2 + (x ^ cross)) * 2 + core) * chunk
            rows = gh_ref[pl.ds(pl.multiple_of(start, chunk), chunk), :] + sent_ref[x, c]
            if x:
                send_ref[c] = rows.astype(send_ref.dtype)
            else:
                kept_ref[c] = rows


def finish_kernel(parts, width, hidden, *refs):
    pieces = refs[:parts]
    (loss_ref, gh_ref, acc_ref) = refs[parts:]
    here = lax.axis_index("ctx")
    blk = acc_ref.shape[1]
    total = None
    for piece, k in zip(pieces, (0,) + RETURN_ORDER):
        owner = here ^ k
        groups = (hidden + width) // LANES
        cuts = [piece[i * blk : (i + 1) * blk, :] for i in range(groups)]
        gh_ref[owner] = jnp.concatenate(cuts[: hidden // LANES], axis=1)
        acc = jnp.concatenate(cuts[hidden // LANES :], axis=1)
        total = acc if total is None else total + acc
        loss_ref[0, pl.ds(owner, 1), :] = piece[groups * blk : groups * blk + 1, :blk]
    acc_ref[0] = total


def acceptor_kernel(blocks, blk, grad_ref, w_ref, slope_ref, out_ref):
    here = lax.axis_index("ctx")
    w = w_ref[...]
    width = w.shape[0]
    total = [None] * blocks
    for tile, (_, a) in enumerate(tiles_of(blocks)):
        grad_pair = lax.dot_general(
            grad_ref[tile], w, (((1,), (1,)), ((), ())), preferred_element_type=jnp.float32
        )
        part = jnp.sum((grad_pair * slope_ref[tile]).reshape(blk, blk, width), axis=0)
        total[a] = part if total[a] is None else total[a] + part
    for a in range(blocks):
        out_ref[a ^ here] = total[a]


def shared(
    donor_feat,
    acceptor_feat,
    donor_pos,
    acceptor_pos,
    pair_mask,
    targets,
    dist_table,
    hidden_weights,
    output_weights,
):
    _, blk, width = donor_feat.shape
    blocks = lax.axis_size("ctx")
    tissues, _, hidden = hidden_weights.shape
    bf16 = jnp.bfloat16
    f32 = jnp.float32
    def placed(value, rows, row, lane=0):
        height, extent = value.shape
        room = ((row, rows - row - height, 0), (lane, width - lane - extent, 0))
        return lax.pad(value, jnp.zeros((), value.dtype), room)

    rows = 3 * blk
    last = 2 * blk
    whole = sum(
        placed(value, rows, row, lane)
        for value, row, lane in (
            (pair_mask[0], last, 0),
            (donor_pos, last, LANES),
            (donor_pos, last + 1, LANES),
            (jnp.transpose(targets, (0, 2, 1))[0], last + 4, LANES),
        )
    )
    row = lax.broadcasted_iota(jnp.int32, whole.shape, 0)
    lane = lax.broadcasted_iota(jnp.int32, whole.shape, 1)
    whole = jnp.where((lane >= LANES) & (row == last), whole >> 8, whole & 255).astype(f32)
    sites = placed(donor_feat[0], rows, 0) + placed(acceptor_feat[0], rows, blk)
    packed = (sites.astype(f32) + whole).astype(bf16)
    base = 0.5 * sum(
        placed(value, BINS + blk, row, lane)
        for value, row, lane in (
            (dist_table, 0, 0),
            (output_weights, BINS, 0),
            (output_weights, BINS + tissues, -width),
        )
    )
    spots = placed(acceptor_pos, BINS + blk, BINS + 2 * tissues)
    spots = spots + placed(acceptor_pos, BINS + blk, BINS + 2 * tissues + 1)
    row = lax.broadcasted_iota(jnp.int32, spots.shape, 0)
    spots = jnp.where(row == BINS + 2 * tissues, spots >> 8, spots & 255)
    base = (base.astype(f32) + spots.astype(f32)).astype(bf16)
    w_in = halved(lax.dynamic_index_in_dim(hidden_weights, lax.axis_index("ctx"), 0, False))
    pieces = [swapped(packed, "ctx", k) for k in GATHER_ORDER]
    tiles = len(tiles_of(blocks))
    chunk = width // (4 * blocks)
    pairs = blk * blk
    partial, sent, loss, grad, slope = pl.pallas_call(
        functools.partial(head_kernel, blocks, blk, width),
        out_shape=(
            jax.ShapeDtypeStruct((width, hidden), f32),
            jax.ShapeDtypeStruct((2, blocks, chunk, hidden), f32),
            jax.ShapeDtypeStruct((blocks, 8, LANES), f32),
            jax.ShapeDtypeStruct((tiles, pairs, hidden), bf16),
            jax.ShapeDtypeStruct((tiles, pairs, width), f32),
        ),
        scratch_shapes=[
            pltpu.VMEM((BINS + 2 * blocks * blk, width), bf16),
            pltpu.VMEM((blocks * blk, width), bf16),
            pltpu.VMEM((tiles, pairs, BINS), bf16),
            pltpu.VMEM((tiles, pairs, width), bf16),
            pltpu.VMEM((tiles, pairs, hidden), bf16),
            pltpu.VMEM((tiles, pairs, hidden), f32),
        ],
        compiler_params=pltpu.CompilerParams(vmem_limit_bytes=32 * 2**20),
        name="head",
    )(base, w_in, packed, *pieces)
    sent = swapped(sent, "rep", 1)
    acc = pl.pallas_call(
        functools.partial(acceptor_kernel, blocks, blk),
        out_shape=jax.ShapeDtypeStruct((blocks, blk, width), f32),
        compiler_params=pltpu.CompilerParams(vmem_limit_bytes=16 * 2**20),
        cost_estimate=pl.CostEstimate(
            flops=2 * tiles * pairs * width * hidden,
            bytes_accessed=tiles * pairs * (2 * hidden + 4 * width),
            transcendentals=0,
        ),
        name="acceptors",
    )(grad, w_in, slope)
    kept, sent = pl.pallas_call(
        functools.partial(core_kernel, blocks),
        out_shape=(
            jax.ShapeDtypeStruct((blocks, chunk, hidden), f32),
            jax.ShapeDtypeStruct((blocks, chunk, hidden), bf16),
        ),
        compiler_params=pltpu.CompilerParams(vmem_limit_bytes=8 * 2**20),
        name="core",
    )(partial, sent)
    sent = swapped(sent, "rep", 2)
    acc = acc + swapped(acc, "tis", 1)
    partial = kept + sent.astype(f32)
    cuts = [part[:, :, i : i + LANES] for part in (partial, acc) for i in range(0, part.shape[2], LANES)]
    send = jnp.concatenate(cuts + [loss], axis=1)
    arrived = [send[0]] + [swapped(send[k], "ctx", k) for k in RETURN_ORDER]
    donor_loss, grad_hidden, grad_acceptor = pl.pallas_call(
        functools.partial(finish_kernel, blocks, width, hidden),
        out_shape=(
            jax.ShapeDtypeStruct((1, tissues, blk), jnp.float32),
            jax.ShapeDtypeStruct((tissues, chunk, hidden), jnp.float32),
            jax.ShapeDtypeStruct((1, blk, width), jnp.float32),
        ),
        compiler_params=pltpu.CompilerParams(vmem_limit_bytes=8 * 2**20),
        name="finish",
    )(*arrived)
    return (jnp.transpose(donor_loss, (0, 2, 1)), grad_hidden, grad_acceptor)


def on_device(*args):
    donor_feat, acceptor_feat, _, _, pair_mask, _, _, hidden_weights, _ = args
    blocks = lax.axis_size("ctx")
    tissues, width, hidden = hidden_weights.shape
    blk = donor_feat.shape[1]
    fits = (
        donor_feat.shape[0] == 1
        and tissues == blocks == 4
        and lax.axis_size("rep") == 4
        and lax.axis_size("tis") == 2
        and acceptor_feat.shape[1] == blk == 16
        and width == 256
        and hidden == 2 * width
        and pair_mask.shape[2] == (SPAN_BLOCKS + 1) * blk
        and BINS == LANES == 2 * blocks * blk
    )
    return shared(*args) if fits else general(*args)


def solution(mesh):
    placed = (
        P("rep", "ctx", None),
        P("rep", "ctx", None),
        P("rep", "ctx"),
        P("rep", None),
        P("rep", "ctx", None),
        P("rep", "ctx", "tis"),
        P(),
        P("tis", None, None),
        P("tis", None),
    )
    return jax.shard_map(
        on_device,
        mesh=mesh,
        in_specs=placed,
        out_specs=(P("rep", "ctx", "tis"), P("tis", ("ctx", "rep"), None), P("rep", "ctx", None)),
        check_vma=False,
    )
```
